32 devices in a mesh: rep: 2 (over y), ep: 8 (over z, core), tp: 2 (over x).
Axes of the slice: x: 2, y: 2, z: 4, core: 2. Of those that a mesh axis runs over, the one named last changes fastest.
Arguments:
- hidden_states: bfloat16 [2, 1024, 2048], P(None, ('rep', 'ep'), 'tp'), parts along dimension 1, may hold values from -8 to 8
- queries: bfloat16 [2, 1024, 4096], P(None, ('rep', 'ep'), 'tp'), parts along dimension 1, may hold values from -8 to 8
- fresh_key_value: bfloat16 [2, 1024, 2, 512], P(None, ('rep', 'ep'), None, 'tp'), parts along dimension 1, may hold values from -8 to 8
- cache: bfloat16 [16, 2, 1024, 512], P(('rep', 'ep'), None, None, 'tp'), parts along dimension 0, may hold values from -8 to 8
- cache_lengths: int32 [16], P(('rep', 'ep')), parts along dimension 0, may hold values from 1 to 1024, 4096 in all
- out_weight: bfloat16 [4096, 2048], P('tp', 'ep'), may hold values from -1 to 1
- router_weight: bfloat16 [2048, 16], P('tp'), may hold values from -0.125 to 0.125
- expert_weights: bfloat16 [16, 3, 2048, 384], P('ep', None, 'tp'), may hold values from -0.21875 to 0.21875
- expert_ids: int32 [2, 1024, 8], P(None, ('rep', 'ep')), parts along dimension 1, may hold values from 0 to 15, all different within a row; in each aligned block of 64 rows (0 to 63, 64 to 127, ..., all dimensions but the last counted through in order) at most 48 rows name the same one
- old_slots: int32 [16], replicated, may hold values from 0 to 15, as said below
- new_slots: int32 [16], replicated, may hold values from 0 to 15, as said below
- moved_experts: int32 [4], replicated, may hold values from 0 to 15, as said below
Outputs:
- mixed: bfloat16 [2, 1024, 2048], P(None, ('rep', 'ep'), 'tp'), parts along dimension 1
The draws below stay inside these ranges and needn't reach their ends.
There are 2 independent parts, one for each index of `rep`. The reference program is written for one: setup_inputs(seed, part) draws one part's arguments, and reference() takes and returns one part's arrays. A program takes and returns all parts, laid end to end along the dimension named above; an argument that names none is the same for every part. Nothing has to cross between parts.
Inputs may be any that keep to these rules, and one draw needn't show every extreme that they name: `expert_ids`: each row names 8 different experts. Within the 64 rows of one request in one token block, no expert is named by more than 48 rows, a bound that some block reaches. `old_slots`: A permutation: each slot holds one expert. `new_slots`: equal to old_slots except at the moved experts, which take one another's old slots, none keeping its own. `moved_experts`: 4 different experts; no two of their old slots s share the same s // 2.
All inputs are finite; a program needn't handle non-finite values. No bound on the sum of `cache_lengths` on one device may be relied on, other than what follows from the above.
Results may differ from the reference program's by a relative error of at most 0.017.
Values may be sent and summed in bfloat16 or wider, within the bound.
No kernel may reach another device: no remote copies, remote signals or barrier semaphores. Data moves between devices by JAX's collectives and lax.ppermute only.
A program may use at most 64 MiB of HBM per device.

```python
import math
import jax
import jax.numpy as jnp
import numpy as np
from jax import lax

D = 2048
QUERY_HEADS = 32
KEY_VALUE_HEADS = 4
HEAD_SIZE = 128
FFW = 384
TOP = 8
EXP_DEV = 2
REQUEST_TOKENS = 64
CACHED_POSITIONS = 1024
EXPERTS = 16
REQUEST_COUNT = 8
BLOCK_TOKENS = 512
CAP = 48
MOVED = 4
QUARTER = 1024
N_TP = 2


def slot_plan(key):
    base_key = jax.random.fold_in(key, 5)
    perm_key, device_key, local_key = jax.random.split(base_key, 3)
    old_table = jax.random.permutation(perm_key, EXPERTS).astype(jnp.int32)
    devices = jax.random.permutation(device_key, REQUEST_COUNT)[:MOVED].astype(jnp.int32)
    local_pick = jax.random.randint(local_key, (MOVED,), 0, EXP_DEV).astype(jnp.int32)
    chosen = (devices * EXP_DEV + local_pick).astype(jnp.int32)
    owners = jnp.argsort(old_table).astype(jnp.int32)
    moved_list = owners[chosen].astype(jnp.int32)
    new_table = old_table.at[moved_list].set(jnp.roll(chosen, -1))
    return (old_table, new_table, moved_list)


def draw_old_slots(key, part):
    return slot_plan(key)[0]


def draw_new_slots(key, part):
    return slot_plan(key)[1]


def draw_moved_experts(key, part):
    return slot_plan(key)[2]


def draw_queries(key, part):
    array_extent = (2, BLOCK_TOKENS, QUERY_HEADS * HEAD_SIZE)
    return jnp.clip(jax.random.normal(jax.random.fold_in(key, 1), array_extent), -8.0, 8.0).astype(jnp.bfloat16)


def draw_fresh_key_value(key, part):
    array_extent = (2, BLOCK_TOKENS, 2, KEY_VALUE_HEADS * HEAD_SIZE)
    return jnp.clip(jax.random.normal(jax.random.fold_in(key, 2), array_extent), -8.0, 8.0).astype(jnp.bfloat16)


def draw_hidden_states(key, part):
    array_extent = (2, BLOCK_TOKENS, D)
    along = jnp.arange(D, dtype=jnp.float32) / (D - 1)
    rough = jnp.exp(jax.random.uniform(jax.random.fold_in(key, 8), (D,), minval=jnp.log(0.7), maxval=jnp.log(1.4)))
    base_values = jax.random.normal(jax.random.fold_in(key, 4), array_extent)
    row_scale = jnp.exp(jax.random.uniform(jax.random.fold_in(key, 7), (2, BLOCK_TOKENS, 1), minval=jnp.log(0.2), maxval=jnp.log(2.0)))
    column_scale = jnp.exp(jnp.log(0.4) + (jnp.log(4.0) - jnp.log(0.4)) * along) * rough
    return jnp.clip(0.5 * base_values * row_scale * column_scale, -8.0, 8.0).astype(jnp.bfloat16)


def level_of(key, dims, cuts, least, high):
    def one(dim, blocks):
        draws = jax.random.uniform(jax.random.fold_in(jax.random.fold_in(key, 6), dim), (blocks,), jnp.float32, least / len(cuts), high / len(cuts))
        return jnp.repeat(jnp.exp(draws), dims[dim] // blocks).reshape((-1,) + (1,) * (len(dims) - dim - 1))

    gain = one(*cuts[0])
    for cut in cuts[1:]:
        gain = gain * one(*cut)
    return gain


def profile(number_of, total, bound, skew):
    portions = [(1 << 20) // math.isqrt(grade ** skew) + 1 for grade in range(2, number_of + 1)]
    spare, counts = total - bound - (number_of - 1), [1] * (number_of - 1)
    while spare > 0:
        candidates = [i for i in range(number_of - 1) if counts[i] < bound]
        mass, remaining = sum([portions[i] for i in candidates]), spare
        for i in candidates:
            more = min(bound - counts[i], max(1, remaining * portions[i] // mass), spare)
            counts[i] = counts[i] + more
            spare = spare - more
    return np.array([bound] + counts)


def ragged_sizes(rng, count, total, bound, lean):
    if count == 2:
        one = jax.random.randint(rng, (), max(1, total - bound), min(bound, total - 1) + 1)
        return jnp.stack([one, total - one])
    sizes = jnp.asarray(profile(count, total, bound, lean), jnp.int32)
    twos = (count - 1) // 2
    giver, receiver = sizes[1:1 + 2 * twos:2], sizes[2:2 + 2 * twos:2]
    margin = jnp.minimum(giver - 1, bound - receiver)
    shifted = jax.random.randint(jax.random.fold_in(rng, 1), (twos,), 0, 1 << 20) % (margin + 1)
    sizes = sizes.at[1:1 + 2 * twos:2].set(giver - shifted).at[2:2 + 2 * twos:2].set(receiver + shifted)
    return sizes[jax.random.permutation(jax.random.fold_in(rng, 2), count)]


def deal_out(rng, own, number, rows, amount, top, most, lean):
    sequence = jax.random.permutation(rng, amount)
    heavy_load, ordinary = portions_of(amount, rows * top, most, lean, True), portions_of(amount, rows * top, most, lean, False)
    places = jnp.arange(amount)

    def named(tallies, rotation):
        used = int((tallies > 0).sum())
        fixed = max(1, used // 4)
        moved = fixed + (places - fixed + rotation * (used - fixed)) % max(1, amount - fixed)
        return jnp.zeros((amount,), jnp.int32).at[sequence[jnp.where(places < fixed, places, moved)]].set(jnp.asarray(tallies, jnp.int32))

    tallies = jnp.where(number % 4 == 0, named(heavy_load, number // 4), named(ordinary, number - number // 4 - 1))
    mixed = jax.random.permutation(jax.random.fold_in(own, 3), amount)
    giver, taker = mixed[0:amount // 2 * 2:2], mixed[1:amount // 2 * 2:2]
    room = jnp.minimum(tallies[giver] - 1, most - tallies[taker]) // 2
    room = jnp.where((giver == sequence[0]) | (taker == sequence[0]) | (tallies[taker] == 0), 0, jnp.maximum(room, 0))
    moved = jax.random.randint(jax.random.fold_in(own, 4), (amount // 2,), 0, 1 << 20) % (room + 1)
    tallies = tallies.at[giver].add(-moved).at[taker].add(moved)
    members = jnp.searchsorted(jnp.cumsum(tallies), jnp.arange(rows * top), side="right").astype(jnp.int32)
    grid = members.reshape(top, rows).T
    grid = grid[jax.random.permutation(jax.random.fold_in(own, 1), rows)]
    rotation = jax.random.randint(jax.random.fold_in(own, 2), (rows, 1), 0, top)
    return jnp.take_along_axis(grid, (jnp.arange(top)[None, :] + rotation) % top, axis=1)


def portions_of(amount, total, bound, slope, full):
    portions = [(1 << 20) // math.isqrt(standing ** slope) + 1 for standing in range(1, amount + 1)]
    largest = bound if full else min(bound, max(-(-total // amount), total * portions[0] // sum(portions)))
    least = 1 if total - largest >= amount - 1 else 0
    holding, surplus = [largest] + [least] * (amount - 1), total - largest - least * (amount - 1)
    while surplus > 0:
        candidates = [i for i in range(1, amount) if holding[i] < largest] or [i for i in range(1, amount) if holding[i] < bound]
        pool, remaining = sum([portions[i] for i in candidates]), surplus
        for i in candidates:
            more = min(bound - holding[i], max(1, remaining * portions[i] // pool), surplus)
            holding[i] = holding[i] + more
            surplus = surplus - more
    return np.array(holding)


def bell_draw(own_key, extent, deviation, limit, cuts=(), kind=jnp.bfloat16):
    values = jax.random.normal(own_key, extent, jnp.float32) * deviation
    if len(cuts) > 0:
        values = level_of(own_key, extent, cuts, -0.22, 0.18) * values
    return jnp.clip(values, min=-limit, max=limit).astype(kind)


def setup_inputs(seed: int = 0, part: int = 0) -> dict:
    key_of = jax.random.split(jax.random.key(seed), 13)
    own_keys = jax.random.split(jax.random.fold_in(key_of[12], part), 13)
    hidden_states = draw_hidden_states(jax.random.fold_in(jax.random.fold_in(key_of[12], part), 71), part)
    queries = draw_queries(jax.random.fold_in(jax.random.fold_in(key_of[12], part), 71), part)
    fresh_key_value = draw_fresh_key_value(jax.random.fold_in(jax.random.fold_in(key_of[12], part), 71), part)
    cache = bell_draw(own_keys[3], (REQUEST_COUNT, 2, CACHED_POSITIONS, KEY_VALUE_HEADS * HEAD_SIZE), 1.0, 8.0, ((0, 8), (3, 2)))
    cache_lengths = ragged_sizes(own_keys[4], REQUEST_COUNT, REQUEST_COUNT * CACHED_POSITIONS // 2, CACHED_POSITIONS, 1).astype(jnp.int32)
    out_weight = bell_draw(key_of[5], (QUERY_HEADS * HEAD_SIZE, D), 0.125, 1.0, ((0, 2), (1, 8)))
    router_weight = bell_draw(key_of[6], (D, EXPERTS), D ** -0.5, 0.125, ((0, 2),))
    expert_weights = bell_draw(key_of[7], (EXPERTS, 3, D, FFW), (2 * FFW) ** -0.5, 0.21875, ((0, 8), (2, 2)))
    expert_ids_keys = jax.random.split(jax.random.fold_in(own_keys[8], 1), 2 * BLOCK_TOKENS // REQUEST_TOKENS)
    expert_ids_turns = jax.random.permutation(jax.random.fold_in(own_keys[8], 3), 2 * BLOCK_TOKENS // REQUEST_TOKENS)
    expert_ids = jax.vmap(lambda own, number: deal_out(jax.random.fold_in(own_keys[8], 2), own, number, REQUEST_TOKENS, EXPERTS, TOP, CAP, 2))(expert_ids_keys, expert_ids_turns).reshape((2, BLOCK_TOKENS, TOP))
    old_slots = draw_old_slots(jax.random.fold_in(key_of[12], 71), part)
    new_slots = draw_new_slots(jax.random.fold_in(key_of[12], 71), part)
    moved_experts = draw_moved_experts(jax.random.fold_in(key_of[12], 71), part)
    return dict(hidden_states=hidden_states, queries=queries, fresh_key_value=fresh_key_value, cache=cache, cache_lengths=cache_lengths, out_weight=out_weight, router_weight=router_weight, expert_weights=expert_weights, expert_ids=expert_ids, old_slots=old_slots, new_slots=new_slots, moved_experts=moved_experts)


def lookup(entries, wanted_keys):
    return lax.optimization_barrier(jnp.sum(jnp.where(wanted_keys[..., None] == jnp.arange(entries.shape[0], dtype=jnp.int32), entries, 0), -1)).astype(jnp.int32)

def slot_source(old_slots, new_slots, moved_experts):
    slots_all = jnp.arange(EXPERTS, dtype=jnp.int32)
    new_moved = lookup(new_slots, moved_experts)
    old_moved = lookup(old_slots, moved_experts)
    matches = slots_all[:, None] == new_moved[None, :]
    return jnp.where(matches.any(1), lax.optimization_barrier(jnp.sum(jnp.where(matches, old_moved[None, :], 0), 1)), slots_all).astype(jnp.int32)

def attend_request(packed):
    query_portion, new_part, cached, length = packed
    row_total = query_portion.shape[1]
    key_matrix = jnp.concatenate([cached[0], new_part[0, :, 0], new_part[1, :, 0]], 0)
    value_matrix = jnp.concatenate([cached[1], new_part[0, :, 1], new_part[1, :, 1]], 0)
    key_total = key_matrix.shape[0]
    query_group_width = QUERY_HEADS // KEY_VALUE_HEADS
    query_matrix = query_portion.reshape(2 * row_total, KEY_VALUE_HEADS, query_group_width, HEAD_SIZE).astype(jnp.float32)
    attention_scores = jnp.einsum('meqt,wet->eqmw', query_matrix, key_matrix.reshape(key_total, KEY_VALUE_HEADS, HEAD_SIZE).astype(jnp.float32)) * HEAD_SIZE ** (-0.5)
    position = jnp.arange(key_total, dtype=jnp.int32)[None, :]
    row_index = jnp.arange(2 * row_total, dtype=jnp.int32)[:, None]
    visible = jnp.where(position < CACHED_POSITIONS, position < length, position - CACHED_POSITIONS <= row_index)
    attention_scores = jnp.where(visible, attention_scores, jnp.float32(-1e+30))
    largest = lax.optimization_barrier(jnp.max(attention_scores, -1, keepdims=True))
    weights = jnp.where(visible, jnp.exp(attention_scores - largest), jnp.float32(0.0))
    route_probability = (weights / lax.optimization_barrier(jnp.sum(weights, -1, keepdims=True))).astype(jnp.bfloat16)
    layer_result = jnp.einsum('qizo,oqx->zqix', route_probability.astype(jnp.float32), value_matrix.reshape(key_total, KEY_VALUE_HEADS, HEAD_SIZE).astype(jnp.float32))
    return layer_result.reshape(2 * row_total, QUERY_HEADS * HEAD_SIZE).astype(jnp.bfloat16)

def expert_block(token_rows, weight):
    row_total = token_rows.shape[0]
    pieces = token_rows.reshape(row_total, N_TP, QUARTER).astype(jnp.float32)
    gate_up_w = weight[:2].reshape(2, N_TP, QUARTER, FFW).astype(jnp.float32)
    partial_value = jnp.einsum('rqc,gqcf->rgqf', pieces, gate_up_w)
    rounded = lax.optimization_barrier(partial_value.astype(jnp.bfloat16)).astype(jnp.float32)
    summed = lax.optimization_barrier(jnp.sum(rounded, 2))
    hidden = (jax.nn.silu(summed[:, 0]) * summed[:, 1]).astype(jnp.bfloat16)
    return jnp.dot(hidden, weight[2].T, preferred_element_type=jnp.float32).astype(jnp.bfloat16)

def mix_block(normed_rows, resid_rows, routed, combine, slot_of_expert, expert_weights):
    expert_marks = (routed[:, :, None] == jnp.arange(EXPERTS, dtype=jnp.int32)[None, None, :]).any(1).astype(jnp.int32)
    grouped = expert_marks.reshape(REQUEST_COUNT, REQUEST_TOKENS, EXPERTS)
    before = (jnp.cumsum(grouped, 1) - grouped).reshape(BLOCK_TOKENS, EXPERTS)
    slot_rank = jnp.take_along_axis(before, routed, 1).astype(jnp.int32)
    block_of = (jnp.arange(BLOCK_TOKENS, dtype=jnp.int32) // REQUEST_TOKENS)[:, None]
    slot_width = REQUEST_COUNT * CAP
    buffer_row = ((routed * REQUEST_COUNT + block_of) * CAP + slot_rank).astype(jnp.int32)
    token_source = jnp.repeat(jnp.arange(BLOCK_TOKENS, dtype=jnp.int32), TOP)
    token_table = jnp.zeros((EXPERTS * slot_width,), jnp.int32).at[buffer_row.reshape(-1)].set(token_source)
    token_table = token_table.reshape(EXPERTS, slot_width)

    def run_expert(expert):
        token_rows = normed_rows[token_table[expert]]
        return expert_block(token_rows, expert_weights[slot_of_expert[expert]])
    outputs = lax.map(run_expert, jnp.arange(EXPERTS, dtype=jnp.int32))
    gathered = outputs.reshape(EXPERTS * slot_width, D)[buffer_row.reshape(-1)].reshape(BLOCK_TOKENS, TOP, D)
    mixed_rows = resid_rows.astype(jnp.float32) + lax.optimization_barrier(jnp.sum(combine[:, :, None] * gathered.astype(jnp.float32), 1))
    return mixed_rows.astype(jnp.bfloat16)

def reference(hidden_states, queries, fresh_key_value, cache, cache_lengths, out_weight, router_weight, expert_weights, expert_ids, old_slots, new_slots, moved_experts):
    query_parts = queries.reshape(2, REQUEST_COUNT, REQUEST_TOKENS, QUERY_HEADS * HEAD_SIZE).transpose(1, 0, 2, 3)
    fresh_pieces_list = fresh_key_value.reshape(2, REQUEST_COUNT, REQUEST_TOKENS, 2, KEY_VALUE_HEADS * HEAD_SIZE).transpose(1, 0, 2, 3, 4)
    attention = lax.map(attend_request, (query_parts, fresh_pieces_list, cache, cache_lengths))
    attention = attention.reshape(REQUEST_COUNT, 2, REQUEST_TOKENS, QUERY_HEADS * HEAD_SIZE).transpose(1, 0, 2, 3).reshape(2 * BLOCK_TOKENS, QUERY_HEADS * HEAD_SIZE)
    attn_out = jnp.dot(attention, out_weight, preferred_element_type=jnp.float32)
    residual = (hidden_states.reshape(2 * BLOCK_TOKENS, D).astype(jnp.float32) + attn_out).astype(jnp.bfloat16)
    wide = residual.astype(jnp.float32)
    squares = lax.optimization_barrier(jnp.sum(wide * wide, 1))
    normed = (wide * lax.rsqrt(squares / D + 1e-06)[:, None]).astype(jnp.bfloat16)
    logits = jnp.dot(normed, router_weight, preferred_element_type=jnp.float32)
    routed = expert_ids.reshape(2 * BLOCK_TOKENS, TOP)
    selected = jnp.take_along_axis(logits, routed, 1)
    raised = jnp.exp(selected)
    combine = raised / lax.optimization_barrier(jnp.sum(raised, 1, keepdims=True))
    first_mix = mix_block(normed[:BLOCK_TOKENS], residual[:BLOCK_TOKENS], routed[:BLOCK_TOKENS], combine[:BLOCK_TOKENS], old_slots, expert_weights)
    source = slot_source(old_slots, new_slots, moved_experts)
    second_slot = lookup(source, new_slots)
    second_mix = mix_block(normed[BLOCK_TOKENS:], residual[BLOCK_TOKENS:], routed[BLOCK_TOKENS:], combine[BLOCK_TOKENS:], second_slot, expert_weights)
    return jnp.stack([first_mix, second_mix])
```

```python
import functools
import math

import jax
import jax.numpy as jnp
from jax import lax
from jax.experimental import pallas as pl
from jax.experimental.pallas import tpu as pltpu
from jax.sharding import PartitionSpec as P

HEAD_SIZE = 128
LANES = 128
CORES = 2
MIB = 1 << 20
BF16 = jnp.bfloat16
F32 = jnp.float32
COST = pl.CostEstimate(flops=1000, bytes_accessed=1000, transcendentals=0)


def whole():
    return pl.BlockSpec(memory_space=pltpu.VMEM)


def scalars():
    return pl.BlockSpec(memory_space=pltpu.SMEM)


def unplaced():
    return pl.BlockSpec(memory_space=pl.ANY)


def params(mib):
    return pltpu.CompilerParams(vmem_limit_bytes=mib * MIB)


def after(array, earlier):
    return lax.optimization_barrier((array, earlier))[0]


def lookup(entries, wanted_keys):
    return jnp.sum(
        jnp.where(
            wanted_keys[..., None] == jnp.arange(entries.shape[0], dtype=jnp.int32), entries, 0
        ),
        -1,
    )


def slot_tables(old_slots, new_slots, moved_experts):
    slots_all = jnp.arange(old_slots.shape[0], dtype=jnp.int32)
    old_moved = lookup(old_slots, moved_experts)
    new_moved = lookup(new_slots, moved_experts)
    matches = slots_all[:, None] == new_moved[None, :]
    source = jnp.where(
        matches.any(1), jnp.sum(jnp.where(matches, old_moved[None, :], 0), 1), slots_all
    )
    return jnp.stack([old_slots, lookup(source, new_slots)])


def attention_kernel(groups, length_ref, q_ref, cache_ref, fresh_ref, out_ref):
    tokens, width = q_ref.shape[1], q_ref.shape[2]
    rows = 2 * tokens
    context = cache_ref.shape[2]
    heads = width // HEAD_SIZE // groups
    fresh_width = fresh_ref.shape[1] // 2
    length = length_ref[0]
    scale = HEAD_SIZE ** (-0.5) * 1.4426950408889634
    past = lax.broadcasted_iota(jnp.int32, (1, context), 1)
    past_bias = jnp.where(past < length, F32(0.0), F32(-1e30))
    fresh_seen = lax.broadcasted_iota(jnp.int32, (rows, rows), 1) <= (
        lax.broadcasted_iota(jnp.int32, (rows, rows), 0)
    )
    fresh_bias = jnp.where(fresh_seen, F32(0.0), F32(-1e30))
    batch = min(4, heads)
    contract_last = (((1,), (1,)), ((), ()))
    for g in range(groups):
        lanes = pl.ds(g * HEAD_SIZE, HEAD_SIZE)
        past_keys = cache_ref[0, 0, :, lanes]
        past_values = cache_ref[0, 1, :, lanes]
        fresh_keys = fresh_ref[:, lanes]
        fresh_values = fresh_ref[:, pl.ds(fresh_width + g * HEAD_SIZE, HEAD_SIZE)]
        for first in range(0, heads, batch):
            columns = [(g * heads + first + h) * HEAD_SIZE for h in range(batch)]
            q = jnp.concatenate(
                [q_ref[:, :, pl.ds(at, HEAD_SIZE)].reshape(rows, HEAD_SIZE) for at in columns], 0
            )
            past_scores = lax.dot_general(
                q, past_keys, contract_last, preferred_element_type=F32
            ) + past_bias
            fresh_scores = lax.dot_general(
                q, fresh_keys, contract_last, preferred_element_type=F32
            )
            fresh_scores = (
                fresh_scores.reshape(batch, rows, rows) + fresh_bias[None]
            ).reshape(batch * rows, rows)
            largest = jnp.maximum(
                jnp.max(past_scores, 1, keepdims=True), jnp.max(fresh_scores, 1, keepdims=True)
            )
            past_weights = jnp.exp2((past_scores - largest) * scale)
            fresh_weights = jnp.exp2((fresh_scores - largest) * scale)
            total = jnp.sum(past_weights, 1, keepdims=True) + jnp.sum(
                fresh_weights, 1, keepdims=True
            )
            result = jnp.dot(
                past_weights.astype(BF16), past_values, preferred_element_type=F32
            ) + jnp.dot(fresh_weights.astype(BF16), fresh_values, preferred_element_type=F32)
            result = (result / total).astype(BF16)
            for h, at in enumerate(columns):
                out_ref[:, pl.ds(at, HEAD_SIZE)] = result[h * rows : (h + 1) * rows]


def attend(lengths, queries, cache, fresh):
    rows = 2 * queries.shape[1]
    return pl.pallas_call(
        functools.partial(attention_kernel, cache.shape[3] // HEAD_SIZE),
        out_shape=jax.ShapeDtypeStruct((rows, queries.shape[2]), BF16),
        in_specs=[scalars(), whole(), whole(), whole()],
        out_specs=whole(),
        compiler_params=params(40),
        cost_estimate=COST,
        name="attention",
    )(lengths, queries, cache, fresh)


def project_kernel(n_tp, place_ref, *refs):
    t, z_hi = place_ref[0], place_ref[5]
    pieces, weights, out_ref = refs[:n_tp], refs[n_tp:-1], refs[-1]
    chunk = pieces[0].shape[0] // n_tp
    rows = []
    for dt in range(n_tp):
        row = pl.multiple_of(lax.rem(t + dt, n_tp) * chunk, chunk)
        rows += [piece[pl.ds(row, chunk), :] for piece in pieces]
    rows = jnp.concatenate(rows, 0)
    at = 0
    for weight in weights:
        span = weight.shape[1]
        out_ref[:, pl.ds(at, span)] = jnp.dot(rows, weight[...], preferred_element_type=F32)
        at += span


def project(n_tp, place, pieces, weights):
    rows = pieces[0].shape[0] // n_tp * len(pieces) * n_tp
    columns = sum(weight.shape[1] for weight in weights)
    return pl.pallas_call(
        functools.partial(project_kernel, n_tp),
        out_shape=jax.ShapeDtypeStruct((rows, columns), F32),
        in_specs=[scalars()] + [whole()] * (len(pieces) + len(weights)),
        out_specs=whole(),
        compiler_params=params(24),
        cost_estimate=COST,
        name="out_projection",
    )(place, *pieces, *weights)


def finish_kernel(n_tp, spans, place_ref, router_ref, *refs):
    t, core, z_lo, z_hi = place_ref[0], place_ref[2], place_ref[4], place_ref[5]
    pieces, refs = refs[:n_tp], refs[n_tp:]
    weight, early, outs = refs[0], refs[1:-n_tp], refs[-n_tp:]
    chunk = pieces[0].shape[0] // n_tp
    rows = []
    for dt in range(n_tp):
        row = pl.multiple_of(lax.rem(t + dt, n_tp) * chunk, chunk)
        rows += [piece[pl.ds(row, chunk), :] for piece in pieces]
    terms = jnp.dot(jnp.concatenate(rows, 0), weight[...], preferred_element_type=F32)
    for out in outs[1:]:
        out[pl.ds(n_tp * chunk, router_ref.shape[0]), :] = router_ref[...]
    span = weight.shape[1]
    for n in range(spans):
        column = 0
        if spans > 1:
            number = ((z_lo ^ (n // CORES)) * CORES) + (core ^ (n % CORES))
            column = pl.multiple_of(number * span, span)
        for i in range(n_tp * n_tp):
            block = pl.ds(i * chunk, chunk)
            if n + 1 == spans:
                value = terms[i * chunk : (i + 1) * chunk]
            else:
                value = early[0][block, pl.ds(n * span, span)]
            dt, dh = i // n_tp, i % n_tp
            at = pl.multiple_of((z_hi ^ dh) * chunk, chunk)
            outs[dt][pl.ds(at, chunk), pl.ds(column, span)] = value.astype(outs[dt].dtype)


def finish(n_tp, place, router, pieces, weight, early):
    columns = weight.shape[1] + sum(array.shape[1] for array in early)
    spans = columns // weight.shape[1]
    rows = pieces[0].shape[0]
    return pl.pallas_call(
        functools.partial(finish_kernel, n_tp, spans),
        out_shape=[jax.ShapeDtypeStruct((rows, columns), F32)]
        + [jax.ShapeDtypeStruct((rows + router.shape[0], columns), BF16)] * (n_tp - 1),
        in_specs=[scalars()] + [whole()] * (2 + len(pieces) + len(early)),
        out_specs=[whole()] * n_tp,
        compiler_params=params(24),
        cost_estimate=COST,
        name="finish_projection",
    )(place, router, *pieces, weight, *early)


def residual_kernel(n_tp, place_ref, keep_ref, *refs):
    t = place_ref[0]
    terms, hidden, out_ref, marked_ref = refs[: n_tp - 1], refs[n_tp - 1 : -2], refs[-2], refs[-1]
    chunk, columns = hidden[0].shape[0], keep_ref.shape[1]
    for beta, piece in enumerate(hidden):
        rows = pl.ds(pl.multiple_of(lax.rem(t - beta + n_tp, n_tp) * chunk, chunk), chunk)
        total = keep_ref[rows, :]
        for term in terms:
            total = total + term[rows, :].astype(F32)
        total = (piece[:, pl.ds(0, columns)].astype(F32) + total).astype(BF16)
        out_ref[rows, :] = total
        marked_ref[rows, pl.ds(0, columns)] = total
        lanes = pl.ds(columns, piece.shape[1] - columns)
        marked_ref[rows, lanes] = piece[:, lanes]


def add_residual(n_tp, place, keep, terms, hidden):
    marked = (keep.shape[0], hidden[0].shape[1])
    return pl.pallas_call(
        functools.partial(residual_kernel, n_tp),
        out_shape=[jax.ShapeDtypeStruct(keep.shape, BF16), jax.ShapeDtypeStruct(marked, BF16)],
        in_specs=[scalars()] + [whole()] * (1 + len(terms) + len(hidden)),
        out_specs=[whole()] * 2,
        compiler_params=params(16),
        cost_estimate=COST,
        name="residual",
    )(place, keep, *terms, *hidden)


def units_kernel(n_tp, n_z, n_rep, place_ref, table_ref, *refs):
    t, z, core, rep = place_ref[0], place_ref[1], place_ref[2], place_ref[3]
    z_lo, z_hi = place_ref[4], place_ref[5]
    m = n_z // n_tp
    routers, pieces, refs = refs[:n_tp], refs[n_tp : n_tp + n_z], refs[n_tp + n_z :]
    own_refs, refs = refs[:CORES], refs[CORES:]
    n_far = CORES * (n_tp - 1) * n_rep
    far_refs, refs = refs[:n_far], refs[n_far:]
    hidden_ref, resid_ref, *outs = refs[:-6]
    normed, chosen_ref, total, near_held, far_held, sems = refs[-6:]
    local, _, quarter, units = own_refs[0].shape
    tokens, width = resid_ref.shape
    chunk = tokens // n_z
    experts = routers[0].shape[0]
    slots = CORES * local

    arriving, later = [[] for _ in range(slots)], []
    for slot in range(slots):
        other, s = slot // local, slot % local
        sources = [(own_refs[other].at[s, pl.ds(0, 2)], near_held.at[slot, pl.ds(0, 2)])]
        for dt in range(1, n_tp):
            for dy in range(n_rep):
                far = far_refs[((dt - 1) * CORES + other) * n_rep + dy]
                size = far.shape[2]
                row = lax.rem(rep + dy, n_rep) * (quarter - size)
                rows = pl.ds(pl.multiple_of(row, math.gcd(size, quarter - size)), size)
                sources.append((far.at[s], far_held.at[dt - 1, slot, :, rows]))
        for n, (source, target) in enumerate(sources):
            copy = pltpu.make_async_copy(source, target, sems.at[slot, n])
            copy.start()
            arriving[slot].append(copy)
    for slot in range(slots):
        copy = pltpu.make_async_copy(
            own_refs[slot // local].at[slot % local, 2], near_held.at[slot, 2], sems.at[slot, len(sources)]
        )
        copy.start()
        later.append(copy)

    for dz in range(n_z):
        row = pl.multiple_of((z_lo ^ (dz % m)) * (n_tp * chunk), n_tp * chunk)
        column = pl.multiple_of((z_hi ^ (dz // m)) * quarter, quarter)
        rows = pl.ds(row, n_tp * chunk)
        resid_ref[rows, pl.ds(column, quarter)] = pieces[dz][:, pl.ds(0, quarter)]
        if dz < m:
            chosen_ref[rows, :] = pieces[dz][:, pl.ds(quarter, chosen_ref.shape[1])]
    wide = resid_ref[...].astype(F32)
    squares = jnp.sum(wide * wide, 1, keepdims=True)
    normed[...] = (wide * lax.rsqrt(squares / width + 1e-06)).astype(BF16)
    logits = jnp.zeros((tokens, experts), F32)
    for dt, router in enumerate(routers):
        at = pl.multiple_of(lax.rem(t - dt + n_tp, n_tp) * quarter, quarter)
        logits = logits + lax.dot_general(
            normed[:, pl.ds(at, quarter)],
            router[pl.ds(router.shape[0] - experts, experts), :],
            (((1,), (1,)), ((), ())),
            preferred_element_type=F32,
        )
    chosen = chosen_ref[:, :experts].astype(F32)
    raised = jnp.where(chosen > 0, jnp.exp(logits), F32(0.0))
    combine = raised / jnp.sum(raised, 1, keepdims=True)

    for slot in range(slots):
        other, s = slot // local, slot % local
        holder = jnp.where(core == 0, other, 1 - other)
        number = (z * CORES + holder) * local + s
        share_of = jnp.sum(
            jnp.where(table_ref[...] == number, combine, F32(0.0)), 1, keepdims=True
        )
        for copy in arriving[slot]:
            copy.wait()
        x = normed[:, pl.ds(pl.multiple_of(t * quarter, quarter), quarter)]
        gate = jnp.dot(x, near_held[slot, 0], preferred_element_type=F32)
        up = jnp.dot(x, near_held[slot, 1], preferred_element_type=F32)
        for dt in range(1, n_tp):
            at = lax.rem(t - dt + n_tp, n_tp) * quarter
            x = normed[:, pl.ds(pl.multiple_of(at, quarter), quarter)]
            gate = gate + jnp.dot(x, far_held[dt - 1, slot, 0], preferred_element_type=F32)
            up = up + jnp.dot(x, far_held[dt - 1, slot, 1], preferred_element_type=F32)
        acted = (gate / (1.0 + jnp.exp(-gate))) * up
        hidden_ref[:, pl.ds(slot * units, units)] = (acted * share_of).astype(BF16)

    for copy in later:
        copy.wait()
    lower([(near_held, slot, 2) for slot in range(slots)], hidden_ref, total, 0)
    resid_lanes = pl.ds(pl.multiple_of(t * quarter, quarter), quarter)
    for dz in range(n_z):
        rows = token_rows(z_lo, z_hi, dz, m, n_tp, chunk)
        value = total[rows, :]
        if dz == 0:
            value = value + resid_ref[rows, resid_lanes].astype(F32)
        outs[dz][...] = value.astype(outs[dz].dtype)


def token_rows(z_lo, z_hi, dz, m, n_tp, chunk):
    at = (z_lo ^ (dz % m)) * n_tp + (z_hi ^ (dz // m))
    return pl.ds(pl.multiple_of(at * chunk, chunk), chunk)


def lower(down, hidden_ref, total, start):
    units = hidden_ref.shape[1] // len(down)
    width = down[0][0].shape[-2]
    step = min(512, width)
    for at in range(0, width, step):
        part = None
        for i, (ref, *index) in enumerate(down):
            term = lax.dot_general(
                hidden_ref[:, pl.ds(i * units, units)],
                ref[(*index, pl.ds(at, step))],
                (((1,), (1,)), ((), ())),
                preferred_element_type=F32,
            )
            part = term if part is None else part + term
        total[:, pl.ds(pl.multiple_of(start + at, step), step)] = part


def features_kernel(n_tp, n_z, dt, place_ref, hidden_ref, resid_ref, *refs):
    t, z_lo, z_hi = place_ref[0], place_ref[4], place_ref[5]
    m = n_z // n_tp
    sources, outs, (total, held, sems) = refs[:-3][: -n_z], refs[:-3][-n_z:], refs[-3:]
    local = sources[0].shape[0]
    parts = len(sources) // CORES
    quarter = total.shape[1]
    chunk = hidden_ref.shape[0] // n_z
    copies, at = [], 0
    for part in range(parts):
        size = sources[part * CORES].shape[2]
        for other in range(CORES):
            copy = pltpu.make_async_copy(
                sources[part * CORES + other].at[:, 0],
                held.at[pl.ds(other * local, local), pl.ds(at, size), :],
                sems.at[part, other],
            )
            copy.start()
            copies.append((copy, at, size))
        at += size
    for part in range(parts):
        for copy, at, size in copies[part * CORES : (part + 1) * CORES]:
            copy.wait()
        down = [(held.at[:, pl.ds(at, size)], slot) for slot in range(CORES * local)]
        lower(down, hidden_ref, total, at)
    resid_lanes = pl.ds(pl.multiple_of(lax.rem(t - dt + n_tp, n_tp) * quarter, quarter), quarter)
    for dz in range(n_z):
        rows = token_rows(z_lo, z_hi, dz, m, n_tp, chunk)
        value = total[rows, :]
        if dz == 0:
            value = value + resid_ref[rows, resid_lanes].astype(F32)
        outs[dz][...] = value.astype(outs[dz].dtype)


def run_units(n_tp, n_rep, place, table, routers, pieces, weights):
    n_z = len(pieces)
    local, _, quarter, units = weights[0].shape
    width = quarter * n_tp
    lanes = pieces[0].shape[1] - quarter
    tokens = pieces[0].shape[0] * (n_z // n_tp)
    part = (tokens // n_z, quarter)
    slots = CORES * local
    found = pl.pallas_call(
        functools.partial(units_kernel, n_tp, n_z, n_rep),
        out_shape=[
            jax.ShapeDtypeStruct((tokens, CORES * local * units), BF16),
            jax.ShapeDtypeStruct((tokens, width), BF16),
        ]
        + [jax.ShapeDtypeStruct(part, BF16 if dz else F32) for dz in range(n_z)],
        in_specs=[scalars()]
        + [whole()] * (1 + n_tp + len(pieces))
        + [unplaced()] * len(weights),
        out_specs=[whole()] * (2 + n_z),
        scratch_shapes=[
            pltpu.VMEM((tokens, width), BF16),
            pltpu.VMEM((tokens, lanes), BF16),
            pltpu.VMEM((tokens, quarter), F32),
            pltpu.VMEM((slots, 3, quarter, units), BF16),
            pltpu.VMEM((n_tp - 1, slots, 2, quarter, units), BF16),
            pltpu.SemaphoreType.DMA((slots, 2 + (n_tp - 1) * n_rep)),
        ],
        compiler_params=params(56),
        cost_estimate=COST,
        name="units",
    )(place, table, *routers, *pieces, *weights)
    return found[0], found[1], found[2:]


def run_features(n_tp, n_z, dt, place, hidden, resid, quarter, weights):
    tokens = hidden.shape[0]
    local = weights[0].shape[0]
    part = (tokens // n_z, quarter)
    return pl.pallas_call(
        functools.partial(features_kernel, n_tp, n_z, dt),
        out_shape=[jax.ShapeDtypeStruct(part, BF16)] * n_z,
        in_specs=[scalars()] + [whole()] * 2 + [unplaced()] * len(weights),
        out_specs=[whole()] * n_z,
        scratch_shapes=[
            pltpu.VMEM((tokens, quarter), F32),
            pltpu.VMEM((CORES * local, quarter, hidden.shape[1] // (CORES * local)), BF16),
            pltpu.SemaphoreType.DMA((len(weights) // CORES, CORES)),
        ],
        compiler_params=params(56),
        cost_estimate=COST,
        name="features",
    )(place, hidden, resid, *weights)


def message_kernel(n_tp, place_ref, hidden_ref, ids_ref, *outs):
    z_hi = place_ref[5]
    chunk, lanes = outs[0].shape[0], outs[0].shape[1] - hidden_ref.shape[1]
    experts = lax.broadcasted_iota(jnp.int32, (chunk, lanes), 1)
    for beta, out_ref in enumerate(outs):
        rows = pl.ds(pl.multiple_of(lax.rem(z_hi + beta, n_tp) * chunk, chunk), chunk)
        ids = ids_ref[rows, :]
        found = jnp.zeros((chunk, lanes), F32)
        for k in range(ids.shape[1]):
            found = found + jnp.where(ids[:, k : k + 1] == experts, F32(1.0), F32(0.0))
        out_ref[:, pl.ds(0, hidden_ref.shape[1])] = hidden_ref[rows, :]
        out_ref[:, pl.ds(hidden_ref.shape[1], lanes)] = found.astype(BF16)


def messages(n_tp, place, hidden, ids, experts):
    shape = (ids.shape[0] // n_tp, hidden.shape[1] + experts + -experts % LANES)
    return pl.pallas_call(
        functools.partial(message_kernel, n_tp),
        out_shape=[jax.ShapeDtypeStruct(shape, BF16)] * n_tp,
        in_specs=[scalars(), whole(), whole()],
        out_specs=[whole()] * n_tp,
        compiler_params=params(16),
        cost_estimate=COST,
        name="messages",
    )(place, hidden, ids)


def mix_kernel(n_tp, n_z, place_ref, *refs):
    t = place_ref[0]
    parts, out_ref = refs[:-1], refs[-1]
    chunk = parts[0].shape[0]
    for dt in range(n_tp):
        value = parts[dt * n_z][...].astype(F32)
        for dz in range(1, n_z):
            value = value + parts[dt * n_z + dz][...].astype(F32)
        row = pl.multiple_of(lax.rem(t + dt, n_tp) * chunk, chunk)
        out_ref[pl.ds(row, chunk), :] = value.astype(BF16)


def mix(n_tp, n_z, place, parts):
    chunk, span = parts[0].shape
    return pl.pallas_call(
        functools.partial(mix_kernel, n_tp, n_z),
        out_shape=jax.ShapeDtypeStruct((chunk * n_tp, span), BF16),
        in_specs=[scalars()] + [whole()] * len(parts),
        out_specs=whole(),
        compiler_params=params(16),
        cost_estimate=COST,
        name="mix",
    )(place, *parts)


def per_device(
    hidden_states,
    queries,
    fresh_key_value,
    cache,
    cache_lengths,
    out_weight,
    router_weight,
    expert_weights,
    expert_ids,
    old_slots,
    new_slots,
    moved_experts,
):
    n_tp, n_ep, n_rep = lax.axis_size("tp"), lax.axis_size("ep"), lax.axis_size("rep")
    n_z = n_ep // CORES
    m = n_z // n_tp
    tokens, quarter = hidden_states.shape[1:]
    rows = 2 * tokens
    chunk = rows // n_tp
    experts = router_weight.shape[1]
    t, e, y = lax.axis_index("tp"), lax.axis_index("ep"), lax.axis_index("rep")
    z, core = e // CORES, e % CORES
    z_hi, z_lo = z // m, z % m
    place = jnp.stack([t, z, core, y, z_lo, z_hi]).astype(jnp.int32)

    def send(array, target):
        pairs = []
        for i in range(n_ep):
            for k in range(n_tp):
                to_ep, to_tp = target(i, k)
                pairs.append((i * n_tp + k, to_ep * n_tp + to_tp % n_tp))
        return lax.ppermute(array, ("ep", "tp"), pairs)

    def to_core(array):
        return lax.ppermute(array, "ep", [(i, i ^ 1) for i in range(n_ep)])

    def to_tp(array, shift):
        return lax.ppermute(array, "tp", [(i, (i + shift) % n_tp) for i in range(n_tp)])

    def to_rep(array, shift):
        return lax.ppermute(array, "rep", [(i, (i + shift) % n_rep) for i in range(n_rep)])

    def to_z(array, dz, dt=0):
        return send(array, lambda i, k: (i ^ (dz * CORES), k + dt))

    def over_z(array, low, high):
        found = {0: array}
        for dz in range(low, high, low):
            step = low
            while not dz & step:
                step *= 2
            found[dz] = to_z(found[dz ^ step], step)
        return [found[dz] for dz in range(0, high, low)]

    def block_of(array, matrices, first_row, size):
        first, last = matrices
        return lax.dynamic_slice(
            array, (0, first, first_row, 0), (array.shape[0], last - first, size, array.shape[3])
        )

    def far(block):
        return [send(block, lambda i, k: (i ^ 1, k + dt)) for dt in range(1, n_tp)]

    near = over_z(out_weight, 1, m)
    out_other = to_core(out_weight)
    share = quarter // n_rep - quarter // 32
    first = far(block_of(expert_weights, (0, 2), y * share, quarter - share))

    queries = after(queries, out_other)
    fresh = fresh_key_value.reshape(rows, -1)
    attention = attend(cache_lengths, queries, cache, fresh)
    pieces = over_z(attention, m, n_z)
    own_other = to_core(expert_weights)
    hidden_states, weights = after((hidden_states, expert_weights), attention)
    outgoing = messages(
        n_tp, place, hidden_states.reshape(rows, quarter), expert_ids.reshape(rows, -1), experts
    )
    blocks = [
        block_of(weights, (2, 3), first * quarter // 4, size * quarter // 4)
        for first, size in ((0, 1), (1, 1), (2, 2))
    ]
    near, old_slots, router, outgoing, blocks, first = after(
        (near, old_slots, router_weight, outgoing, blocks, first), (pieces[1], own_other)
    )
    router = router.T
    tables = slot_tables(old_slots, new_slots, moved_experts)
    table = lax.dynamic_slice_in_dim(tables, t * chunk // tokens, 1, 0)
    crossed = [out_other] + [to_core(array) for array in near[1:]]
    early = [array for pair in zip(near, crossed) for array in pair]
    last = early.pop()
    if out_weight.shape[1] % LANES:
        order = (jnp.arange(m)[:, None] ^ z_lo) * CORES + (jnp.arange(CORES) ^ core)
        together = jnp.stack(early + [last])[order.reshape(-1)]
        last, early = together.transpose(1, 0, 2).reshape(together.shape[1], -1), []
    else:
        early = [project(n_tp, place, pieces, early)]
    hidden = [
        send(
            block,
            lambda i, k: (
                (m * k + (i // CORES) % m) * CORES + i % CORES,
                (i // CORES) // m + beta,
            ),
        )
        for beta, block in enumerate(outgoing)
    ]
    last = after(last, hidden[0])
    sums = finish(n_tp, place, router, pieces, last, early)
    terms = [to_tp(sums[dt], dt) for dt in range(1, n_tp)]
    first_other = [to_core(array) for array in after(first, sums)]
    first = after(first, terms)
    passed = [
        to_rep(lax.dynamic_slice_in_dim(array, y * (quarter - 2 * share), share, 2), 1)
        for array in first
    ]

    resid, marked = add_residual(n_tp, place, sums[0], after(terms, first_other), hidden)
    near = over_z(marked, 1, m)
    wide = to_z(resid, m)
    blocks = after(blocks, resid)
    down = [far(blocks[0])]
    wide, blocks = after((wide, blocks), (wide, near, down))
    down.append(far(blocks[1]))
    gathered = near + [wide]
    for dz in range(m + 1, n_z):
        step = dz & -dz
        gathered.append(to_z(gathered[dz ^ step] if dz ^ step else resid, step))
    gathered, blocks = after((gathered, blocks), (gathered, down))
    down.append(far(blocks[2]))

    passed = after(passed, gathered)
    passed_other = [to_core(array) for array in passed]
    weights = [expert_weights, own_other]
    for dt in range(n_tp - 1):
        weights += [first_other[dt], passed_other[dt], first[dt], passed[dt]]
    units, resid_all, own_parts = run_units(
        n_tp, n_rep, place, table, [router] + terms, gathered, weights
    )
    parts = [own_parts[0]] + [to_z(own_parts[dz], dz) for dz in range(1, n_z)]
    down = after(down, units)
    for dt in range(1, n_tp):
        sources = []
        for arrays in down:
            sources += [to_core(arrays[dt - 1]), arrays[dt - 1]]
        found = run_features(n_tp, n_z, dt, place, units, resid_all, quarter, sources)
        parts += [to_z(found[dz], dz, n_tp - dt) for dz in range(n_z)]
    return mix(n_tp, n_z, place, parts).reshape(2, tokens, quarter)


def solution(mesh):
    return jax.shard_map(
        per_device,
        mesh=mesh,
        in_specs=(
            P(None, ("rep", "ep"), "tp"),
            P(None, ("rep", "ep"), "tp"),
            P(None, ("rep", "ep"), None, "tp"),
            P(("rep", "ep"), None, None, "tp"),
            P(("rep", "ep")),
            P("tp", "ep"),
            P("tp", None),
            P("ep", None, "tp", None),
            P(None, ("rep", "ep"), None),
            P(),
            P(),
            P(),
        ),
        out_specs=P(None, ("rep", "ep"), "tp"),
        check_vma=False,
    )
```

```python
import functools
import math

import jax
import jax.numpy as jnp
from jax import lax
from jax.experimental import pallas as pl
from jax.experimental.pallas import tpu as pltpu
from jax.sharding import PartitionSpec as P

HEAD_SIZE = 128
LANES = 128
CORES = 2
MIB = 1 << 20
BF16 = jnp.bfloat16
F32 = jnp.float32
COST = pl.CostEstimate(flops=1000, bytes_accessed=1000, transcendentals=0)


def whole():
    return pl.BlockSpec(memory_space=pltpu.VMEM)


def scalars():
    return pl.BlockSpec(memory_space=pltpu.SMEM)


def unplaced():
    return pl.BlockSpec(memory_space=pl.ANY)


def params(mib):
    return pltpu.CompilerParams(vmem_limit_bytes=mib * MIB)


def after(array, earlier):
    return lax.optimization_barrier((array, earlier))[0]


def lookup(entries, wanted_keys):
    return jnp.sum(
        jnp.where(
            wanted_keys[..., None] == jnp.arange(entries.shape[0], dtype=jnp.int32), entries, 0
        ),
        -1,
    )


def slot_tables(old_slots, new_slots, moved_experts):
    slots_all = jnp.arange(old_slots.shape[0], dtype=jnp.int32)
    old_moved = lookup(old_slots, moved_experts)
    new_moved = lookup(new_slots, moved_experts)
    matches = slots_all[:, None] == new_moved[None, :]
    source = jnp.where(
        matches.any(1), jnp.sum(jnp.where(matches, old_moved[None, :], 0), 1), slots_all
    )
    return jnp.stack([old_slots, lookup(source, new_slots)])


def attention_kernel(groups, length_ref, q_ref, cache_ref, fresh_ref, out_ref):
    tokens, width = q_ref.shape[1], q_ref.shape[2]
    rows = 2 * tokens
    context = cache_ref.shape[2]
    heads = width // HEAD_SIZE // groups
    fresh_width = fresh_ref.shape[1] // 2
    length = length_ref[0]
    scale = HEAD_SIZE ** (-0.5) * 1.4426950408889634
    past = lax.broadcasted_iota(jnp.int32, (1, context), 1)
    past_bias = jnp.where(past < length, F32(0.0), F32(-1e30))
    fresh_seen = lax.broadcasted_iota(jnp.int32, (rows, rows), 1) <= (
        lax.broadcasted_iota(jnp.int32, (rows, rows), 0)
    )
    fresh_bias = jnp.where(fresh_seen, F32(0.0), F32(-1e30))
    batch = min(4, heads)
    contract_last = (((1,), (1,)), ((), ()))
    for g in range(groups):
        lanes = pl.ds(g * HEAD_SIZE, HEAD_SIZE)
        past_keys = cache_ref[0, 0, :, lanes]
        past_values = cache_ref[0, 1, :, lanes]
        fresh_keys = fresh_ref[:, lanes]
        fresh_values = fresh_ref[:, pl.ds(fresh_width + g * HEAD_SIZE, HEAD_SIZE)]
        for first in range(0, heads, batch):
            columns = [(g * heads + first + h) * HEAD_SIZE for h in range(batch)]
            q = jnp.concatenate(
                [q_ref[:, :, pl.ds(at, HEAD_SIZE)].reshape(rows, HEAD_SIZE) for at in columns], 0
            )
            past_scores = lax.dot_general(
                q, past_keys, contract_last, preferred_element_type=F32
            ) + past_bias
            fresh_scores = lax.dot_general(
                q, fresh_keys, contract_last, preferred_element_type=F32
            )
            fresh_scores = (
                fresh_scores.reshape(batch, rows, rows) + fresh_bias[None]
            ).reshape(batch * rows, rows)
            largest = jnp.maximum(
                jnp.max(past_scores, 1, keepdims=True), jnp.max(fresh_scores, 1, keepdims=True)
            )
            past_weights = jnp.exp2((past_scores - largest) * scale)
            fresh_weights = jnp.exp2((fresh_scores - largest) * scale)
            total = jnp.sum(past_weights, 1, keepdims=True) + jnp.sum(
                fresh_weights, 1, keepdims=True
            )
            result = jnp.dot(
                past_weights.astype(BF16), past_values, preferred_element_type=F32
            ) + jnp.dot(fresh_weights.astype(BF16), fresh_values, preferred_element_type=F32)
            result = (result / total).astype(BF16)
            for h, at in enumerate(columns):
                out_ref[:, pl.ds(at, HEAD_SIZE)] = result[h * rows : (h + 1) * rows]


def attend(lengths, queries, cache, fresh):
    rows = 2 * queries.shape[1]
    return pl.pallas_call(
        functools.partial(attention_kernel, cache.shape[3] // HEAD_SIZE),
        out_shape=jax.ShapeDtypeStruct((rows, queries.shape[2]), BF16),
        in_specs=[scalars(), whole(), whole(), whole()],
        out_specs=whole(),
        compiler_params=params(40),
        cost_estimate=COST,
        name="attention",
    )(lengths, queries, cache, fresh)


def project_kernel(n_tp, place_ref, *refs):
    t, z_hi = place_ref[0], place_ref[5]
    pieces, weights, out_ref = refs[:n_tp], refs[n_tp:-1], refs[-1]
    chunk = pieces[0].shape[0] // n_tp
    rows = []
    for dt in range(n_tp):
        row = pl.multiple_of(lax.rem(t + dt, n_tp) * chunk, chunk)
        rows += [piece[pl.ds(row, chunk), :] for piece in pieces]
    rows = jnp.concatenate(rows, 0)
    at = 0
    for weight in weights:
        span = weight.shape[1]
        out_ref[:, pl.ds(at, span)] = jnp.dot(rows, weight[...], preferred_element_type=F32)
        at += span


def project(n_tp, place, pieces, weights):
    rows = pieces[0].shape[0] // n_tp * len(pieces) * n_tp
    columns = sum(weight.shape[1] for weight in weights)
    return pl.pallas_call(
        functools.partial(project_kernel, n_tp),
        out_shape=jax.ShapeDtypeStruct((rows, columns), F32),
        in_specs=[scalars()] + [whole()] * (len(pieces) + len(weights)),
        out_specs=whole(),
        compiler_params=params(24),
        cost_estimate=COST,
        name="out_projection",
    )(place, *pieces, *weights)


def finish_kernel(n_tp, spans, place_ref, router_ref, *refs):
    t, core, z_lo, z_hi = place_ref[0], place_ref[2], place_ref[4], place_ref[5]
    pieces, refs = refs[:n_tp], refs[n_tp:]
    weight, early, outs = refs[0], refs[1:-n_tp], refs[-n_tp:]
    chunk = pieces[0].shape[0] // n_tp
    rows = []
    for dt in range(n_tp):
        row = pl.multiple_of(lax.rem(t + dt, n_tp) * chunk, chunk)
        rows += [piece[pl.ds(row, chunk), :] for piece in pieces]
    terms = jnp.dot(jnp.concatenate(rows, 0), weight[...], preferred_element_type=F32)
    for out in outs[1:]:
        out[pl.ds(n_tp * chunk, router_ref.shape[0]), :] = router_ref[...]
    span = weight.shape[1]
    for n in range(spans):
        column = 0
        if spans > 1:
            number = ((z_lo ^ (n // CORES)) * CORES) + (core ^ (n % CORES))
            column = pl.multiple_of(number * span, span)
        for i in range(n_tp * n_tp):
            block = pl.ds(i * chunk, chunk)
            if n + 1 == spans:
                value = terms[i * chunk : (i + 1) * chunk]
            else:
                value = early[0][block, pl.ds(n * span, span)]
            dt, dh = i // n_tp, i % n_tp
            at = pl.multiple_of((z_hi ^ dh) * chunk, chunk)
            outs[dt][pl.ds(at, chunk), pl.ds(column, span)] = value.astype(outs[dt].dtype)


def finish(n_tp, place, router, pieces, weight, early):
    columns = weight.shape[1] + sum(array.shape[1] for array in early)
    spans = columns // weight.shape[1]
    rows = pieces[0].shape[0]
    return pl.pallas_call(
        functools.partial(finish_kernel, n_tp, spans),
        out_shape=[jax.ShapeDtypeStruct((rows, columns), F32)]
        + [jax.ShapeDtypeStruct((rows + router.shape[0], columns), BF16)] * (n_tp - 1),
        in_specs=[scalars()] + [whole()] * (2 + len(pieces) + len(early)),
        out_specs=[whole()] * n_tp,
        compiler_params=params(24),
        cost_estimate=COST,
        name="finish_projection",
    )(place, router, *pieces, weight, *early)


def residual_kernel(n_tp, place_ref, keep_ref, *refs):
    z_hi = place_ref[5]
    terms, hidden, out_ref, marked_ref = refs[: n_tp - 1], refs[n_tp - 1 : -2], refs[-2], refs[-1]
    chunk, columns = hidden[0].shape[0], keep_ref.shape[1]
    for dh, piece in enumerate(hidden):
        rows = pl.ds(pl.multiple_of((z_hi ^ dh) * chunk, chunk), chunk)
        total = keep_ref[rows, :]
        for term in terms:
            total = total + term[rows, :].astype(F32)
        total = (piece[:, pl.ds(0, columns)].astype(F32) + total).astype(BF16)
        out_ref[rows, :] = total
        marked_ref[rows, pl.ds(0, columns)] = total
        lanes = pl.ds(columns, piece.shape[1] - columns)
        marked_ref[rows, lanes] = piece[:, lanes]


def add_residual(n_tp, place, keep, terms, hidden):
    marked = (keep.shape[0], hidden[0].shape[1])
    return pl.pallas_call(
        functools.partial(residual_kernel, n_tp),
        out_shape=[jax.ShapeDtypeStruct(keep.shape, BF16), jax.ShapeDtypeStruct(marked, BF16)],
        in_specs=[scalars()] + [whole()] * (1 + len(terms) + len(hidden)),
        out_specs=[whole()] * 2,
        compiler_params=params(16),
        cost_estimate=COST,
        name="residual",
    )(place, keep, *terms, *hidden)


def units_kernel(n_tp, n_z, n_rep, place_ref, table_ref, *refs):
    t, z, core, rep = place_ref[0], place_ref[1], place_ref[2], place_ref[3]
    z_lo, z_hi = place_ref[4], place_ref[5]
    m = n_z // n_tp
    routers, pieces, refs = refs[:n_tp], refs[n_tp : n_tp + n_z], refs[n_tp + n_z :]
    own_refs, refs = refs[:CORES], refs[CORES:]
    n_far = CORES * (n_tp - 1) * n_rep
    far_refs, refs = refs[:n_far], refs[n_far:]
    hidden_ref, resid_ref, *outs = refs[:-6]
    normed, chosen_ref, total, near_held, far_held, sems = refs[-6:]
    local, _, quarter, units = own_refs[0].shape
    tokens, width = resid_ref.shape
    chunk = tokens // n_z
    experts = routers[0].shape[0]
    slots = CORES * local

    arriving, later = [[] for _ in range(slots)], []
    for slot in range(slots):
        other, s = slot // local, slot % local
        sources = [(own_refs[other].at[s, pl.ds(0, 2)], near_held.at[slot, pl.ds(0, 2)])]
        for dt in range(1, n_tp):
            for dy in range(n_rep):
                far = far_refs[((dt - 1) * CORES + other) * n_rep + dy]
                size = far.shape[2]
                row = lax.rem(rep + dy, n_rep) * (quarter - size)
                rows = pl.ds(pl.multiple_of(row, math.gcd(size, quarter - size)), size)
                sources.append((far.at[s], far_held.at[dt - 1, slot, :, rows]))
        for n, (source, target) in enumerate(sources):
            copy = pltpu.make_async_copy(source, target, sems.at[slot, n])
            copy.start()
            arriving[slot].append(copy)
    for slot in range(slots):
        copy = pltpu.make_async_copy(
            own_refs[slot // local].at[slot % local, 2], near_held.at[slot, 2], sems.at[slot, len(sources)]
        )
        copy.start()
        later.append(copy)

    for dz in range(n_z):
        row = pl.multiple_of((z_lo ^ (dz % m)) * (n_tp * chunk), n_tp * chunk)
        column = pl.multiple_of((z_hi ^ (dz // m)) * quarter, quarter)
        rows = pl.ds(row, n_tp * chunk)
        resid_ref[rows, pl.ds(column, quarter)] = pieces[dz][:, pl.ds(0, quarter)]
        if dz < m:
            chosen_ref[rows, :] = pieces[dz][:, pl.ds(quarter, chosen_ref.shape[1])]
    wide = resid_ref[...].astype(F32)
    squares = jnp.sum(wide * wide, 1, keepdims=True)
    normed[...] = (wide * lax.rsqrt(squares / width + 1e-06)).astype(BF16)
    logits = jnp.zeros((tokens, experts), F32)
    for dt, router in enumerate(routers):
        at = pl.multiple_of(lax.rem(t - dt + n_tp, n_tp) * quarter, quarter)
        logits = logits + lax.dot_general(
            normed[:, pl.ds(at, quarter)],
            router[pl.ds(router.shape[0] - experts, experts), :],
            (((1,), (1,)), ((), ())),
            preferred_element_type=F32,
        )
    chosen = chosen_ref[:, :experts].astype(F32)
    raised = jnp.where(chosen > 0, jnp.exp(logits), F32(0.0))
    combine = raised / jnp.sum(raised, 1, keepdims=True)

    for slot in range(slots):
        other, s = slot // local, slot % local
        holder = jnp.where(core == 0, other, 1 - other)
        number = (z * CORES + holder) * local + s
        share_of = jnp.sum(
            jnp.where(table_ref[...] == number, combine, F32(0.0)), 1, keepdims=True
        )
        for copy in arriving[slot]:
            copy.wait()
        x = normed[:, pl.ds(pl.multiple_of(t * quarter, quarter), quarter)]
        gate = jnp.dot(x, near_held[slot, 0], preferred_element_type=F32)
        up = jnp.dot(x, near_held[slot, 1], preferred_element_type=F32)
        for dt in range(1, n_tp):
            at = lax.rem(t - dt + n_tp, n_tp) * quarter
            x = normed[:, pl.ds(pl.multiple_of(at, quarter), quarter)]
            gate = gate + jnp.dot(x, far_held[dt - 1, slot, 0], preferred_element_type=F32)
            up = up + jnp.dot(x, far_held[dt - 1, slot, 1], preferred_element_type=F32)
        acted = (gate / (1.0 + jnp.exp(-gate))) * up
        hidden_ref[:, pl.ds(slot * units, units)] = (acted * share_of).astype(BF16)

    for copy in later:
        copy.wait()
    lower([(near_held, slot, 2) for slot in range(slots)], hidden_ref, total, 0)
    resid_lanes = pl.ds(pl.multiple_of(t * quarter, quarter), quarter)
    for dz in range(n_z):
        rows = token_rows(z_lo, z_hi, dz, m, n_tp, chunk)
        value = total[rows, :]
        if dz == 0:
            value = value + resid_ref[rows, resid_lanes].astype(F32)
        outs[dz][...] = value.astype(outs[dz].dtype)


def token_rows(z_lo, z_hi, dz, m, n_tp, chunk):
    at = (z_lo ^ (dz % m)) * n_tp + (z_hi ^ (dz // m))
    return pl.ds(pl.multiple_of(at * chunk, chunk), chunk)


def lower(down, hidden_ref, total, start):
    units = hidden_ref.shape[1] // len(down)
    width = down[0][0].shape[-2]
    step = min(512, width)
    for at in range(0, width, step):
        part = None
        for i, (ref, *index) in enumerate(down):
            term = lax.dot_general(
                hidden_ref[:, pl.ds(i * units, units)],
                ref[(*index, pl.ds(at, step))],
                (((1,), (1,)), ((), ())),
                preferred_element_type=F32,
            )
            part = term if part is None else part + term
        total[:, pl.ds(pl.multiple_of(start + at, step), step)] = part


def features_kernel(n_tp, n_z, dt, place_ref, hidden_ref, resid_ref, *refs):
    t, z_lo, z_hi = place_ref[0], place_ref[4], place_ref[5]
    m = n_z // n_tp
    sources, outs, (total, held, sems) = refs[:-3][: -n_z], refs[:-3][-n_z:], refs[-3:]
    local = sources[0].shape[0]
    parts = len(sources) // CORES
    quarter = total.shape[1]
    chunk = hidden_ref.shape[0] // n_z
    copies, at = [], 0
    for part in range(parts):
        size = sources[part * CORES].shape[2]
        for other in range(CORES):
            copy = pltpu.make_async_copy(
                sources[part * CORES + other].at[:, 0],
                held.at[pl.ds(other * local, local), pl.ds(at, size), :],
                sems.at[part, other],
            )
            copy.start()
            copies.append((copy, at, size))
        at += size
    for part in range(parts):
        for copy, at, size in copies[part * CORES : (part + 1) * CORES]:
            copy.wait()
        down = [(held.at[:, pl.ds(at, size)], slot) for slot in range(CORES * local)]
        lower(down, hidden_ref, total, at)
    resid_lanes = pl.ds(pl.multiple_of(lax.rem(t - dt + n_tp, n_tp) * quarter, quarter), quarter)
    for dz in range(n_z):
        rows = token_rows(z_lo, z_hi, dz, m, n_tp, chunk)
        value = total[rows, :]
        if dz == 0:
            value = value + resid_ref[rows, resid_lanes].astype(F32)
        outs[dz][...] = value.astype(outs[dz].dtype)


def run_units(n_tp, n_rep, place, table, routers, pieces, weights):
    n_z = len(pieces)
    local, _, quarter, units = weights[0].shape
    width = quarter * n_tp
    lanes = pieces[0].shape[1] - quarter
    tokens = pieces[0].shape[0] * (n_z // n_tp)
    part = (tokens // n_z, quarter)
    slots = CORES * local
    found = pl.pallas_call(
        functools.partial(units_kernel, n_tp, n_z, n_rep),
        out_shape=[
            jax.ShapeDtypeStruct((tokens, CORES * local * units), BF16),
            jax.ShapeDtypeStruct((tokens, width), BF16),
        ]
        + [jax.ShapeDtypeStruct(part, BF16 if dz else F32) for dz in range(n_z)],
        in_specs=[scalars()]
        + [whole()] * (1 + n_tp + len(pieces))
        + [unplaced()] * len(weights),
        out_specs=[whole()] * (2 + n_z),
        scratch_shapes=[
            pltpu.VMEM((tokens, width), BF16),
            pltpu.VMEM((tokens, lanes), BF16),
            pltpu.VMEM((tokens, quarter), F32),
            pltpu.VMEM((slots, 3, quarter, units), BF16),
            pltpu.VMEM((n_tp - 1, slots, 2, quarter, units), BF16),
            pltpu.SemaphoreType.DMA((slots, 2 + (n_tp - 1) * n_rep)),
        ],
        compiler_params=params(56),
        cost_estimate=COST,
        name="units",
    )(place, table, *routers, *pieces, *weights)
    return found[0], found[1], found[2:]


def run_features(n_tp, n_z, dt, place, hidden, resid, quarter, weights):
    tokens = hidden.shape[0]
    local = weights[0].shape[0]
    part = (tokens // n_z, quarter)
    return pl.pallas_call(
        functools.partial(features_kernel, n_tp, n_z, dt),
        out_shape=[jax.ShapeDtypeStruct(part, BF16)] * n_z,
        in_specs=[scalars()] + [whole()] * 2 + [unplaced()] * len(weights),
        out_specs=[whole()] * n_z,
        scratch_shapes=[
            pltpu.VMEM((tokens, quarter), F32),
            pltpu.VMEM((CORES * local, quarter, hidden.shape[1] // (CORES * local)), BF16),
            pltpu.SemaphoreType.DMA((len(weights) // CORES, CORES)),
        ],
        compiler_params=params(56),
        cost_estimate=COST,
        name="features",
    )(place, hidden, resid, *weights)


def message_kernel(n_tp, place_ref, hidden_ref, ids_ref, *refs):
    t, z_hi = place_ref[0], place_ref[5]
    swapped, outs = refs[: n_tp - 1], refs[n_tp - 1 :]
    columns = hidden_ref.shape[1]
    chunk, lanes = outs[0].shape[0], outs[0].shape[1] - columns
    experts = lax.broadcasted_iota(jnp.int32, (chunk, lanes), 1)
    rows = pl.ds(pl.multiple_of(t * chunk, chunk), chunk)
    ids = ids_ref[rows, :]
    found = jnp.zeros((chunk, lanes), F32)
    for k in range(ids.shape[1]):
        found = found + jnp.where(ids[:, k : k + 1] == experts, F32(1.0), F32(0.0))
    for dh, out_ref in enumerate(outs):
        value = hidden_ref[rows, :]
        for dt in range(1, n_tp):
            source = lax.rem(t - dt + n_tp, n_tp)
            value = jnp.where(source == (z_hi ^ dh), swapped[dt - 1][...], value)
        out_ref[:, pl.ds(0, columns)] = value
        out_ref[:, pl.ds(columns, lanes)] = found.astype(BF16)


def messages(n_tp, place, hidden, ids, swapped, experts):
    shape = (ids.shape[0] // n_tp, hidden.shape[1] + experts + -experts % LANES)
    return pl.pallas_call(
        functools.partial(message_kernel, n_tp),
        out_shape=[jax.ShapeDtypeStruct(shape, BF16)] * n_tp,
        in_specs=[scalars()] + [whole()] * (2 + len(swapped)),
        out_specs=[whole()] * n_tp,
        compiler_params=params(16),
        cost_estimate=COST,
        name="messages",
    )(place, hidden, ids, *swapped)


def mix_kernel(n_tp, n_z, place_ref, *refs):
    t = place_ref[0]
    parts, out_ref = refs[:-1], refs[-1]
    chunk = parts[0].shape[0]
    for dt in range(n_tp):
        value = parts[dt * n_z][...].astype(F32)
        for dz in range(1, n_z):
            value = value + parts[dt * n_z + dz][...].astype(F32)
        row = pl.multiple_of(lax.rem(t + dt, n_tp) * chunk, chunk)
        out_ref[pl.ds(row, chunk), :] = value.astype(BF16)


def mix(n_tp, n_z, place, parts):
    chunk, span = parts[0].shape
    return pl.pallas_call(
        functools.partial(mix_kernel, n_tp, n_z),
        out_shape=jax.ShapeDtypeStruct((chunk * n_tp, span), BF16),
        in_specs=[scalars()] + [whole()] * len(parts),
        out_specs=whole(),
        compiler_params=params(16),
        cost_estimate=COST,
        name="mix",
    )(place, *parts)


def per_device(
    hidden_states,
    queries,
    fresh_key_value,
    cache,
    cache_lengths,
    out_weight,
    router_weight,
    expert_weights,
    expert_ids,
    old_slots,
    new_slots,
    moved_experts,
):
    n_tp, n_ep, n_rep = lax.axis_size("tp"), lax.axis_size("ep"), lax.axis_size("rep")
    n_z = n_ep // CORES
    m = n_z // n_tp
    tokens, quarter = hidden_states.shape[1:]
    rows = 2 * tokens
    chunk = rows // n_tp
    experts = router_weight.shape[1]
    t, e, y = lax.axis_index("tp"), lax.axis_index("ep"), lax.axis_index("rep")
    z, core = e // CORES, e % CORES
    z_hi, z_lo = z // m, z % m
    place = jnp.stack([t, z, core, y, z_lo, z_hi]).astype(jnp.int32)

    def send(array, target):
        pairs = []
        for i in range(n_ep):
            for k in range(n_tp):
                to_ep, to_tp = target(i, k)
                pairs.append((i * n_tp + k, to_ep * n_tp + to_tp % n_tp))
        return lax.ppermute(array, ("ep", "tp"), pairs)

    def to_core(array):
        return lax.ppermute(array, "ep", [(i, i ^ 1) for i in range(n_ep)])

    def to_tp(array, shift):
        return lax.ppermute(array, "tp", [(i, (i + shift) % n_tp) for i in range(n_tp)])

    def to_rep(array, shift):
        return lax.ppermute(array, "rep", [(i, (i + shift) % n_rep) for i in range(n_rep)])

    def to_z(array, dz, dt=0):
        return send(array, lambda i, k: (i ^ (dz * CORES), k + dt))

    def over_z(array, low, high):
        found = {0: array}
        for dz in range(low, high, low):
            step = low
            while not dz & step:
                step *= 2
            found[dz] = to_z(found[dz ^ step], step)
        return [found[dz] for dz in range(0, high, low)]

    def block_of(array, matrices, first_row, size):
        first, last = matrices
        return lax.dynamic_slice(
            array, (0, first, first_row, 0), (array.shape[0], last - first, size, array.shape[3])
        )

    def far(block):
        return [send(block, lambda i, k: (i ^ 1, k + dt)) for dt in range(1, n_tp)]

    flat_hidden = hidden_states.reshape(rows, quarter)
    swapped = [
        to_tp(
            lax.dynamic_slice_in_dim(flat_hidden, lax.rem(t + dt, n_tp) * chunk, chunk, 0), dt
        )
        for dt in range(1, n_tp)
    ]
    near = over_z(out_weight, 1, m)
    out_other = to_core(out_weight)
    share = quarter // n_rep
    first = far(after(block_of(expert_weights, (0, 2), y * share, share), swapped))

    queries = after(queries, (out_other, swapped))
    fresh = fresh_key_value.reshape(rows, -1)
    attention = attend(cache_lengths, queries, cache, fresh)
    pieces = over_z(attention, m, n_z)
    own_other = to_core(expert_weights)
    expert_ids, weights, old_slots, router = after(
        (expert_ids, expert_weights, old_slots, router_weight), attention
    )
    outgoing = messages(
        n_tp, place, flat_hidden, expert_ids.reshape(rows, -1), swapped, experts
    )
    blocks = [block_of(weights, (2, 3), n * quarter // 2, quarter // 2) for n in range(2)]
    router = router.T
    tables = slot_tables(old_slots, new_slots, moved_experts)
    table = lax.dynamic_slice_in_dim(tables, t * chunk // tokens, 1, 0)
    near, table, router, outgoing, blocks, first = after(
        (near, table, router, outgoing, blocks, first), (pieces[1], own_other)
    )
    hidden = [outgoing[0]] + [to_z(outgoing[dh], dh * m) for dh in range(1, n_tp)]
    passed = [to_rep(array, 1) for array in first]
    crossed = [out_other] + [to_core(array) for array in near[1:]]
    early = [array for pair in zip(near, crossed) for array in pair]
    last = early.pop()
    if out_weight.shape[1] % LANES:
        order = (jnp.arange(m)[:, None] ^ z_lo) * CORES + (jnp.arange(CORES) ^ core)
        together = jnp.stack(early + [last])[order.reshape(-1)]
        last, early = together.transpose(1, 0, 2).reshape(together.shape[1], -1), []
    else:
        early = [project(n_tp, place, pieces, early)]
    sums = finish(n_tp, place, router, pieces, last, early)
    terms = [to_tp(sums[dt], dt) for dt in range(1, n_tp)]
    first = after(first, sums)
    first_other = [to_core(array) for array in first]

    resid, marked = add_residual(n_tp, place, sums[0], after(terms, first_other), hidden)
    near = over_z(marked, 1, m)
    wide = to_z(resid, m)
    blocks = after(blocks, resid)
    down = [far(blocks[0])]
    wide = after(wide, near)
    gathered = near + [wide]
    for dz in range(m + 1, n_z):
        step = dz & -dz
        gathered.append(to_z(gathered[dz ^ step] if dz ^ step else resid, step))
    gathered, blocks = after((gathered, blocks), (gathered, down))
    down.append(far(blocks[1]))

    passed = after(passed, gathered)
    passed_other = [to_core(array) for array in passed]
    weights = [expert_weights, own_other]
    for dt in range(n_tp - 1):
        weights += [first_other[dt], passed_other[dt], first[dt], passed[dt]]
    units, resid_all, own_parts = run_units(
        n_tp, n_rep, place, table, [router] + terms, gathered, weights
    )
    parts = [own_parts[0]] + [to_z(own_parts[dz], dz) for dz in range(1, n_z)]
    down = after(down, units)
    for dt in range(1, n_tp):
        sources = []
        for arrays in down:
            sources += [to_core(arrays[dt - 1]), arrays[dt - 1]]
        found = run_features(n_tp, n_z, dt, place, units, resid_all, quarter, sources)
        parts += [to_z(found[dz], dz, n_tp - dt) for dz in range(n_z)]
    return mix(n_tp, n_z, place, parts).reshape(2, tokens, quarter)


def solution(mesh):
    return jax.shard_map(
        per_device,
        mesh=mesh,
        in_specs=(
            P(None, ("rep", "ep"), "tp"),
            P(None, ("rep", "ep"), "tp"),
            P(None, ("rep", "ep"), None, "tp"),
            P(("rep", "ep"), None, None, "tp"),
            P(("rep", "ep")),
            P("tp", "ep"),
            P("tp", None),
            P("ep", None, "tp", None),
            P(None, ("rep", "ep"), None),
            P(),
            P(),
            P(),
        ),
        out_specs=P(None, ("rep", "ep"), "tp"),
        check_vma=False,
    )
```

```python
import functools
import math

import jax
import jax.numpy as jnp
from jax import lax
from jax.experimental import pallas as pl
from jax.experimental.pallas import tpu as pltpu
from jax.sharding import PartitionSpec as P

HEAD_SIZE = 128
LANES = 128
CORES = 2
MIB = 1 << 20
BF16 = jnp.bfloat16
F32 = jnp.float32
COST = pl.CostEstimate(flops=1000, bytes_accessed=1000, transcendentals=0)


def whole():
    return pl.BlockSpec(memory_space=pltpu.VMEM)


def scalars():
    return pl.BlockSpec(memory_space=pltpu.SMEM)


def unplaced():
    return pl.BlockSpec(memory_space=pltpu.HBM)


def params(mib):
    return pltpu.CompilerParams(vmem_limit_bytes=mib * MIB)


def after(array, earlier):
    return lax.optimization_barrier((array, earlier))[0]


def lookup(entries, wanted_keys):
    return jnp.sum(
        jnp.where(
            wanted_keys[..., None] == jnp.arange(entries.shape[0], dtype=jnp.int32), entries, 0
        ),
        -1,
    )


def slot_tables(old_slots, new_slots, moved_experts):
    slots_all = jnp.arange(old_slots.shape[0], dtype=jnp.int32)
    old_moved = lookup(old_slots, moved_experts)
    new_moved = lookup(new_slots, moved_experts)
    matches = slots_all[:, None] == new_moved[None, :]
    source = jnp.where(
        matches.any(1), jnp.sum(jnp.where(matches, old_moved[None, :], 0), 1), slots_all
    )
    return jnp.stack([old_slots, lookup(source, new_slots)])


def attention_kernel(groups, length_ref, q_ref, cache_ref, fresh_ref, out_ref):
    tokens, width = q_ref.shape[1], q_ref.shape[2]
    rows = 2 * tokens
    context = cache_ref.shape[2]
    heads = width // HEAD_SIZE // groups
    fresh_width = fresh_ref.shape[1] // 2
    length = length_ref[0]
    scale = HEAD_SIZE ** (-0.5) * 1.4426950408889634
    past = lax.broadcasted_iota(jnp.int32, (1, context), 1)
    past_bias = jnp.where(past < length, F32(0.0), F32(-1e30))
    fresh_seen = lax.broadcasted_iota(jnp.int32, (rows, rows), 1) <= (
        lax.broadcasted_iota(jnp.int32, (rows, rows), 0)
    )
    fresh_bias = jnp.where(fresh_seen, F32(0.0), F32(-1e30))
    batch = min(4, heads)
    contract_last = (((1,), (1,)), ((), ()))
    for g in range(groups):
        lanes = pl.ds(g * HEAD_SIZE, HEAD_SIZE)
        past_keys = cache_ref[0, 0, :, lanes]
        past_values = cache_ref[0, 1, :, lanes]
        fresh_keys = fresh_ref[:, lanes]
        fresh_values = fresh_ref[:, pl.ds(fresh_width + g * HEAD_SIZE, HEAD_SIZE)]
        for first in range(0, heads, batch):
            columns = [(g * heads + first + h) * HEAD_SIZE for h in range(batch)]
            q = jnp.concatenate(
                [q_ref[:, :, pl.ds(at, HEAD_SIZE)].reshape(rows, HEAD_SIZE) for at in columns], 0
            )
            past_scores = lax.dot_general(
                q, past_keys, contract_last, preferred_element_type=F32
            ) + past_bias
            fresh_scores = lax.dot_general(
                q, fresh_keys, contract_last, preferred_element_type=F32
            )
            fresh_scores = (
                fresh_scores.reshape(batch, rows, rows) + fresh_bias[None]
            ).reshape(batch * rows, rows)
            largest = jnp.maximum(
                jnp.max(past_scores, 1, keepdims=True), jnp.max(fresh_scores, 1, keepdims=True)
            )
            past_weights = jnp.exp2((past_scores - largest) * scale)
            fresh_weights = jnp.exp2((fresh_scores - largest) * scale)
            total = jnp.sum(past_weights, 1, keepdims=True) + jnp.sum(
                fresh_weights, 1, keepdims=True
            )
            result = jnp.dot(
                past_weights.astype(BF16), past_values, preferred_element_type=F32
            ) + jnp.dot(fresh_weights.astype(BF16), fresh_values, preferred_element_type=F32)
            result = (result / total).astype(BF16)
            for h, at in enumerate(columns):
                out_ref[:, pl.ds(at, HEAD_SIZE)] = result[h * rows : (h + 1) * rows]


def attend(lengths, queries, cache, fresh):
    rows = 2 * queries.shape[1]
    return pl.pallas_call(
        functools.partial(attention_kernel, cache.shape[3] // HEAD_SIZE),
        out_shape=jax.ShapeDtypeStruct((rows, queries.shape[2]), BF16),
        in_specs=[scalars(), whole(), whole(), whole()],
        out_specs=whole(),
        compiler_params=params(40),
        cost_estimate=COST,
        name="attention",
    )(lengths, queries, cache, fresh)


def project_kernel(n_tp, place_ref, *refs):
    t, z_hi = place_ref[0], place_ref[5]
    pieces, weights, out_ref = refs[:n_tp], refs[n_tp:-1], refs[-1]
    chunk = pieces[0].shape[0] // n_tp
    rows = []
    for dt in range(n_tp):
        row = pl.multiple_of(lax.rem(t + dt, n_tp) * chunk, chunk)
        rows += [piece[pl.ds(row, chunk), :] for piece in pieces]
    rows = jnp.concatenate(rows, 0)
    at = 0
    for weight in weights:
        span = weight.shape[1]
        out_ref[:, pl.ds(at, span)] = jnp.dot(rows, weight[...], preferred_element_type=F32)
        at += span


def project(n_tp, place, pieces, weights):
    rows = pieces[0].shape[0] // n_tp * len(pieces) * n_tp
    columns = sum(weight.shape[1] for weight in weights)
    return pl.pallas_call(
        functools.partial(project_kernel, n_tp),
        out_shape=jax.ShapeDtypeStruct((rows, columns), F32),
        in_specs=[scalars()] + [whole()] * (len(pieces) + len(weights)),
        out_specs=whole(),
        compiler_params=params(24),
        cost_estimate=COST,
        name="out_projection",
    )(place, *pieces, *weights)


def finish_kernel(n_tp, spans, place_ref, router_ref, *refs):
    t, core, z_lo, z_hi = place_ref[0], place_ref[2], place_ref[4], place_ref[5]
    pieces, refs = refs[:n_tp], refs[n_tp:]
    weight, early, outs = refs[0], refs[1:-n_tp], refs[-n_tp:]
    chunk = pieces[0].shape[0] // n_tp
    rows = []
    for dt in range(n_tp):
        row = pl.multiple_of(lax.rem(t + dt, n_tp) * chunk, chunk)
        rows += [piece[pl.ds(row, chunk), :] for piece in pieces]
    terms = jnp.dot(jnp.concatenate(rows, 0), weight[...], preferred_element_type=F32)
    for out in outs[1:]:
        out[pl.ds(n_tp * chunk, router_ref.shape[0]), :] = router_ref[...]
    span = weight.shape[1]
    for n in range(spans):
        column = 0
        if spans > 1:
            number = ((z_lo ^ (n // CORES)) * CORES) + (core ^ (n % CORES))
            column = pl.multiple_of(number * span, span)
        for i in range(n_tp * n_tp):
            block = pl.ds(i * chunk, chunk)
            if n + 1 == spans:
                value = terms[i * chunk : (i + 1) * chunk]
            else:
                value = early[0][block, pl.ds(n * span, span)]
            dt, dh = i // n_tp, i % n_tp
            at = pl.multiple_of((z_hi ^ dh) * chunk, chunk)
            outs[dt][pl.ds(at, chunk), pl.ds(column, span)] = value.astype(outs[dt].dtype)


def finish(n_tp, place, router, pieces, weight, early):
    columns = weight.shape[1] + sum(array.shape[1] for array in early)
    spans = columns // weight.shape[1]
    rows = pieces[0].shape[0]
    return pl.pallas_call(
        functools.partial(finish_kernel, n_tp, spans),
        out_shape=[jax.ShapeDtypeStruct((rows, columns), F32)]
        + [jax.ShapeDtypeStruct((rows + router.shape[0], columns), BF16)] * (n_tp - 1),
        in_specs=[scalars()] + [whole()] * (2 + len(pieces) + len(early)),
        out_specs=[whole()] * n_tp,
        compiler_params=params(24),
        cost_estimate=COST,
        name="finish_projection",
    )(place, router, *pieces, weight, *early)


def residual_kernel(n_tp, place_ref, keep_ref, *refs):
    z_hi = place_ref[5]
    terms, hidden, out_ref, marked_ref = refs[: n_tp - 1], refs[n_tp - 1 : -2], refs[-2], refs[-1]
    chunk, columns = hidden[0].shape[0], keep_ref.shape[1]
    for dh, piece in enumerate(hidden):
        rows = pl.ds(pl.multiple_of((z_hi ^ dh) * chunk, chunk), chunk)
        total = keep_ref[rows, :]
        for term in terms:
            total = total + term[rows, :].astype(F32)
        total = (piece[:, pl.ds(0, columns)].astype(F32) + total).astype(BF16)
        out_ref[rows, :] = total
        marked_ref[rows, pl.ds(0, columns)] = total
        lanes = pl.ds(columns, piece.shape[1] - columns)
        marked_ref[rows, lanes] = piece[:, lanes]


def add_residual(n_tp, place, keep, terms, hidden):
    marked = (keep.shape[0], hidden[0].shape[1])
    return pl.pallas_call(
        functools.partial(residual_kernel, n_tp),
        out_shape=[jax.ShapeDtypeStruct(keep.shape, BF16), jax.ShapeDtypeStruct(marked, BF16)],
        in_specs=[scalars()] + [whole()] * (1 + len(terms) + len(hidden)),
        out_specs=[whole()] * 2,
        compiler_params=params(16),
        cost_estimate=COST,
        name="residual",
    )(place, keep, *terms, *hidden)


def hold_kernel(count, *refs):
    sems = refs[-1]
    copies = [
        pltpu.make_async_copy(refs[n], refs[count + n], sems.at[n]) for n in range(count)
    ]
    for copy in copies:
        copy.start()
    for copy in copies:
        copy.wait()


def hold(arrays):
    return pl.pallas_call(
        functools.partial(hold_kernel, len(arrays)),
        out_shape=[pltpu.VMEM(array.shape, array.dtype) for array in arrays],
        in_specs=[unplaced()] * len(arrays),
        out_specs=[whole()] * len(arrays),
        scratch_shapes=[pltpu.SemaphoreType.DMA((len(arrays),))],
        compiler_params=params(2),
        cost_estimate=COST,
        name="hold",
    )(*arrays)


def units_kernel(n_tp, n_z, n_rep, place_ref, table_ref, *refs):
    t, z, core, rep = place_ref[0], place_ref[1], place_ref[2], place_ref[3]
    z_lo, z_hi = place_ref[4], place_ref[5]
    m = n_z // n_tp
    routers, pieces, refs = refs[:n_tp], refs[n_tp : n_tp + n_z], refs[n_tp + n_z :]
    own_refs, refs = refs[:CORES], refs[CORES:]
    n_far = CORES * (n_tp - 1)
    first_refs, passed_refs, refs = refs[:n_far], refs[n_far : 2 * n_far], refs[2 * n_far :]
    hidden_ref, far_resid_ref, *outs = refs[:-6]
    resid_ref, normed, chosen_ref, total, passed_held, sems = refs[-6:]
    local, _, quarter, units = own_refs[0].shape
    tokens, width = resid_ref.shape
    chunk = tokens // n_z
    experts = routers[0].shape[0]

    arriving = []
    for n in range(n_far):
        copy = pltpu.make_async_copy(passed_refs[n], passed_held.at[n], sems.at[n])
        copy.start()
        arriving.append(copy)

    for dz in range(n_z):
        row = pl.multiple_of((z_lo ^ (dz % m)) * (n_tp * chunk), n_tp * chunk)
        column = pl.multiple_of((z_hi ^ (dz // m)) * quarter, quarter)
        rows = pl.ds(row, n_tp * chunk)
        resid_ref[rows, pl.ds(column, quarter)] = pieces[dz][:, pl.ds(0, quarter)]
        if dz < m:
            chosen_ref[rows, :] = pieces[dz][:, pl.ds(quarter, chosen_ref.shape[1])]
    wide = resid_ref[...].astype(F32)
    squares = jnp.sum(wide * wide, 1, keepdims=True)
    normed[...] = (wide * lax.rsqrt(squares / width + 1e-06)).astype(BF16)
    logits = jnp.zeros((tokens, experts), F32)
    for dt, router in enumerate(routers):
        at = pl.multiple_of(lax.rem(t - dt + n_tp, n_tp) * quarter, quarter)
        logits = logits + lax.dot_general(
            normed[:, pl.ds(at, quarter)],
            router[pl.ds(router.shape[0] - experts, experts), :],
            (((1,), (1,)), ((), ())),
            preferred_element_type=F32,
        )
    chosen = chosen_ref[:, :experts].astype(F32)
    raised = jnp.where(chosen > 0, jnp.exp(logits), F32(0.0))
    combine = raised / jnp.sum(raised, 1, keepdims=True)

    shares = []
    for slot in range(CORES * local):
        other, s = slot // local, slot % local
        holder = jnp.where(core == 0, other, 1 - other)
        number = (z * CORES + holder) * local + s
        shares.append(
            jnp.sum(jnp.where(table_ref[...] == number, combine, F32(0.0)), 1, keepdims=True)
        )
    share = quarter // n_rep
    near = normed[:, pl.ds(pl.multiple_of(t * quarter, quarter), quarter)]
    for other in range(CORES):
        for copy in arriving[other * (n_tp - 1) : (other + 1) * (n_tp - 1)]:
            copy.wait()
        for s in range(local):
            both = []
            for matrix in range(2):
                terms = jnp.dot(near, own_refs[other][s, matrix], preferred_element_type=F32)
                for dt in range(1, n_tp):
                    n = other * (n_tp - 1) + dt - 1
                    base = lax.rem(t - dt + n_tp, n_tp) * quarter
                    for dy, ref in ((0, first_refs[n]), (1, passed_held.at[n])):
                        at = base + lax.rem(rep + dy, n_rep) * share
                        x = normed[:, pl.ds(pl.multiple_of(at, share), share)]
                        terms = terms + jnp.dot(x, ref[s, matrix], preferred_element_type=F32)
                both.append(terms)
            gate, up = both
            acted = (gate / (1.0 + jnp.exp(-gate))) * up
            slot = other * local + s
            hidden_ref[:, pl.ds(slot * units, units)] = (acted * shares[slot]).astype(BF16)

    down = [(own_refs[slot // local], slot % local, 2) for slot in range(CORES * local)]
    lower(down, hidden_ref, total, 0, quarter)
    resid_lanes = pl.ds(pl.multiple_of(t * quarter, quarter), quarter)
    for dz in range(n_z):
        rows = token_rows(z_lo, z_hi, dz, m, n_tp, chunk)
        value = total[rows, :]
        if dz == 0:
            value = value + resid_ref[rows, resid_lanes].astype(F32)
        outs[dz][...] = value.astype(outs[dz].dtype)
    own_rows = token_rows(z_lo, z_hi, 0, m, n_tp, chunk)
    for dt in range(1, n_tp):
        lanes = pl.multiple_of(lax.rem(t - dt + n_tp, n_tp) * quarter, quarter)
        far_resid_ref[dt - 1] = resid_ref[own_rows, pl.ds(lanes, quarter)]


def token_rows(z_lo, z_hi, dz, m, n_tp, chunk):
    at = (z_lo ^ (dz % m)) * n_tp + (z_hi ^ (dz // m))
    return pl.ds(pl.multiple_of(at * chunk, chunk), chunk)


def lower(down, hidden_ref, total, start, width):
    units = hidden_ref.shape[1] // len(down)
    step = min(512, width)
    for at in range(0, width, step):
        size = min(step, width - at)
        part = None
        for i, (ref, *index) in enumerate(down):
            term = lax.dot_general(
                hidden_ref[:, pl.ds(i * units, units)],
                ref[(*index, pl.ds(at, size))],
                (((1,), (1,)), ((), ())),
                preferred_element_type=F32,
            )
            part = term if part is None else part + term
        total[:, pl.ds(start + at, size)] = part


def features_kernel(n_tp, n_z, dt, place_ref, hidden_ref, resid_ref, *refs):
    z_lo, z_hi = place_ref[4], place_ref[5]
    m = n_z // n_tp
    sources, refs = refs[: 2 * CORES], refs[2 * CORES :]
    outs, total, helds, sems = refs[:n_z], refs[n_z], refs[n_z + 1 : -1], refs[-1]
    local = sources[0].shape[0]
    chunk = hidden_ref.shape[0] // n_z
    copies = []
    for n, source in enumerate(sources):
        copy = pltpu.make_async_copy(source, helds[n // CORES].at[n % CORES], sems.at[n])
        copy.start()
        copies.append(copy)
    start = 0
    for n, held in enumerate(helds):
        for copy in copies[n * CORES : (n + 1) * CORES]:
            copy.wait()
        down = [(held.at[slot // local], slot % local, 0) for slot in range(CORES * local)]
        lower(down, hidden_ref, total, start, held.shape[3])
        start += held.shape[3]
    for dz in range(n_z):
        value = total[token_rows(z_lo, z_hi, dz, m, n_tp, chunk), :]
        if dz == 0:
            value = value + resid_ref[dt - 1].astype(F32)
        outs[dz][...] = value.astype(outs[dz].dtype)


def run_units(n_tp, n_rep, place, table, routers, pieces, own, first, passed):
    n_z = len(pieces)
    local, _, quarter, units = own[0].shape
    width = quarter * n_tp
    lanes = pieces[0].shape[1] - quarter
    tokens = pieces[0].shape[0] * (n_z // n_tp)
    part = (tokens // n_z, quarter)
    slots = CORES * local
    n_far = CORES * (n_tp - 1)
    found = pl.pallas_call(
        functools.partial(units_kernel, n_tp, n_z, n_rep),
        out_shape=[
            pltpu.VMEM((tokens, slots * units), BF16),
            jax.ShapeDtypeStruct((n_tp - 1, *part), BF16),
        ]
        + [jax.ShapeDtypeStruct(part, BF16 if dz else F32) for dz in range(n_z)],
        in_specs=[scalars()]
        + [whole()] * (1 + n_tp + len(pieces) + len(own) + len(first))
        + [unplaced()] * n_far,
        out_specs=[whole()] * (2 + n_z),
        scratch_shapes=[
            pltpu.VMEM((tokens, width), BF16),
            pltpu.VMEM((tokens, width), BF16),
            pltpu.VMEM((tokens, lanes), BF16),
            pltpu.VMEM((tokens, quarter), F32),
            pltpu.VMEM((n_far, *passed[0].shape), BF16),
            pltpu.SemaphoreType.DMA((n_far,)),
        ],
        compiler_params=params(28),
        cost_estimate=COST,
        name="units",
    )(place, table, *routers, *pieces, *own, *first, *passed)
    return found[0], found[1], found[2:]


def run_features(n_tp, n_z, dt, place, hidden, resid, weights):
    tokens = hidden.shape[0]
    part = resid.shape[1:]
    return pl.pallas_call(
        functools.partial(features_kernel, n_tp, n_z, dt),
        out_shape=[jax.ShapeDtypeStruct(part, BF16)] * n_z,
        in_specs=[scalars()] + [whole()] * 2 + [unplaced()] * len(weights),
        out_specs=[whole()] * n_z,
        scratch_shapes=[
            pltpu.VMEM((tokens, part[1]), F32),
            *[pltpu.VMEM((CORES, *array.shape), BF16) for array in weights[::CORES]],
            pltpu.SemaphoreType.DMA((len(weights),)),
        ],
        compiler_params=params(16),
        cost_estimate=COST,
        name="features",
    )(place, hidden, resid, *weights)


def message_kernel(n_tp, place_ref, hidden_ref, ids_ref, *refs):
    t, z_hi = place_ref[0], place_ref[5]
    swapped, outs = refs[: n_tp - 1], refs[n_tp - 1 :]
    columns = hidden_ref.shape[1]
    chunk, lanes = outs[0].shape[0], outs[0].shape[1] - columns
    experts = lax.broadcasted_iota(jnp.int32, (chunk, lanes), 1)
    rows = pl.ds(pl.multiple_of(t * chunk, chunk), chunk)
    ids = ids_ref[rows, :]
    found = jnp.zeros((chunk, lanes), F32)
    for k in range(ids.shape[1]):
        found = found + jnp.where(ids[:, k : k + 1] == experts, F32(1.0), F32(0.0))
    for dh, out_ref in enumerate(outs):
        value = hidden_ref[rows, :]
        for dt in range(1, n_tp):
            source = lax.rem(t - dt + n_tp, n_tp)
            value = jnp.where(source == (z_hi ^ dh), swapped[dt - 1][...], value)
        out_ref[:, pl.ds(0, columns)] = value
        out_ref[:, pl.ds(columns, lanes)] = found.astype(BF16)


def messages(n_tp, place, hidden, ids, swapped, experts):
    shape = (ids.shape[0] // n_tp, hidden.shape[1] + experts + -experts % LANES)
    return pl.pallas_call(
        functools.partial(message_kernel, n_tp),
        out_shape=[jax.ShapeDtypeStruct(shape, BF16)] * n_tp,
        in_specs=[scalars()] + [whole()] * (2 + len(swapped)),
        out_specs=[whole()] * n_tp,
        compiler_params=params(16),
        cost_estimate=COST,
        name="messages",
    )(place, hidden, ids, *swapped)


def mix_kernel(n_tp, n_z, place_ref, *refs):
    t = place_ref[0]
    parts, out_ref = refs[:-1], refs[-1]
    chunk = parts[0].shape[0]
    for dt in range(n_tp):
        value = parts[dt * n_z][...].astype(F32)
        for dz in range(1, n_z):
            value = value + parts[dt * n_z + dz][...].astype(F32)
        row = pl.multiple_of(lax.rem(t + dt, n_tp) * chunk, chunk)
        out_ref[pl.ds(row, chunk), :] = value.astype(BF16)


def mix(n_tp, n_z, place, parts):
    chunk, span = parts[0].shape
    return pl.pallas_call(
        functools.partial(mix_kernel, n_tp, n_z),
        out_shape=jax.ShapeDtypeStruct((chunk * n_tp, span), BF16),
        in_specs=[scalars()] + [whole()] * len(parts),
        out_specs=whole(),
        compiler_params=params(16),
        cost_estimate=COST,
        name="mix",
    )(place, *parts)


def per_device(
    hidden_states,
    queries,
    fresh_key_value,
    cache,
    cache_lengths,
    out_weight,
    router_weight,
    expert_weights,
    expert_ids,
    old_slots,
    new_slots,
    moved_experts,
):
    n_tp, n_ep, n_rep = lax.axis_size("tp"), lax.axis_size("ep"), lax.axis_size("rep")
    n_z = n_ep // CORES
    m = n_z // n_tp
    tokens, quarter = hidden_states.shape[1:]
    rows = 2 * tokens
    chunk = rows // n_tp
    experts = router_weight.shape[1]
    t, e, y = lax.axis_index("tp"), lax.axis_index("ep"), lax.axis_index("rep")
    z, core = e // CORES, e % CORES
    z_hi, z_lo = z // m, z % m
    place = jnp.stack([t, z, core, y, z_lo, z_hi]).astype(jnp.int32)

    def send(array, target):
        pairs = []
        for i in range(n_ep):
            for k in range(n_tp):
                to_ep, to_tp = target(i, k)
                pairs.append((i * n_tp + k, to_ep * n_tp + to_tp % n_tp))
        return lax.ppermute(array, ("ep", "tp"), pairs)

    def to_core(array):
        return lax.ppermute(array, "ep", [(i, i ^ 1) for i in range(n_ep)])

    def to_tp(array, shift):
        return lax.ppermute(array, "tp", [(i, (i + shift) % n_tp) for i in range(n_tp)])

    def to_rep(array, shift):
        return lax.ppermute(array, "rep", [(i, (i + shift) % n_rep) for i in range(n_rep)])

    def to_z(array, dz, dt=0):
        return send(array, lambda i, k: (i ^ (dz * CORES), k + dt))

    def over_z(array, low, high):
        found = {0: array}
        for dz in range(low, high, low):
            step = low
            while not dz & step:
                step *= 2
            found[dz] = to_z(found[dz ^ step], step)
        return [found[dz] for dz in range(0, high, low)]

    def block_of(array, matrices, first_row, size):
        first, last = matrices
        return lax.dynamic_slice(
            array, (0, first, first_row, 0), (array.shape[0], last - first, size, array.shape[3])
        )

    def far(block):
        return [send(block, lambda i, k: (i ^ 1, k + dt)) for dt in range(1, n_tp)]

    flat_hidden = hidden_states.reshape(rows, quarter)
    swapped = [
        to_tp(
            lax.dynamic_slice_in_dim(flat_hidden, lax.rem(t + dt, n_tp) * chunk, chunk, 0), dt
        )
        for dt in range(1, n_tp)
    ]
    near = over_z(out_weight, 1, m)
    out_other = to_core(out_weight)
    share = quarter // n_rep
    first = far(after(block_of(expert_weights, (0, 2), y * share, share), swapped))

    queries = after(queries, (out_other, swapped))
    fresh = fresh_key_value.reshape(rows, -1)
    attention = attend(cache_lengths, queries, cache, fresh)
    pieces = over_z(attention, m, n_z)
    own_other = to_core(expert_weights)
    own = hold(after([expert_weights, own_other], attention))
    expert_ids, weights, old_slots, router = after(
        (expert_ids, expert_weights, old_slots, router_weight), own
    )
    outgoing = messages(
        n_tp, place, flat_hidden, expert_ids.reshape(rows, -1), swapped, experts
    )
    edge = max(LANES, 5 * quarter // 8 // LANES * LANES)
    blocks = [
        block_of(weights, (2, 3), first_row, last_row - first_row)
        for first_row, last_row in ((0, edge), (edge, quarter))
    ]
    router = router.T
    tables = slot_tables(old_slots, new_slots, moved_experts)
    table = lax.dynamic_slice_in_dim(tables, t * chunk // tokens, 1, 0)
    near, table, router, outgoing, blocks, first = after(
        (near, table, router, outgoing, blocks, first), (pieces[1], own)
    )
    hidden = [outgoing[0]] + [to_z(outgoing[dh], dh * m) for dh in range(1, n_tp)]
    passed = [to_rep(array, 1) for array in first]
    crossed = [out_other] + [to_core(array) for array in near[1:]]
    early = [array for pair in zip(near, crossed) for array in pair]
    last = early.pop()
    if out_weight.shape[1] % LANES:
        order = (jnp.arange(m)[:, None] ^ z_lo) * CORES + (jnp.arange(CORES) ^ core)
        together = jnp.stack(early + [last])[order.reshape(-1)]
        last, early = together.transpose(1, 0, 2).reshape(together.shape[1], -1), []
    else:
        early = [project(n_tp, place, pieces, early)]
    sums = finish(n_tp, place, router, pieces, last, early)
    terms = [to_tp(sums[dt], dt) for dt in range(1, n_tp)]
    first = after(first, sums)
    first_other = [to_core(array) for array in first]

    resid, marked = add_residual(n_tp, place, sums[0], after(terms, first_other), hidden)
    near = over_z(marked, 1, m)
    wide = to_z(resid, m)
    blocks = after(blocks, resid)
    down = [far(blocks[0])]
    held = hold(after(first_other + first, resid))
    wide = after(wide, (near, held))
    gathered = near + [wide]
    for dz in range(m + 1, n_z):
        step = dz & -dz
        gathered.append(to_z(gathered[dz ^ step] if dz ^ step else resid, step))
    gathered, blocks = after((gathered, blocks), (gathered, down))
    down.append(far(blocks[1]))

    passed, down[0] = after((passed, down[0]), gathered)
    passed_other = [to_core(array) for array in passed]
    units, far_resid, own_parts = run_units(
        n_tp,
        n_rep,
        place,
        table,
        [router] + terms,
        gathered,
        own,
        held,
        passed_other + passed,
    )
    parts = [own_parts[0]] + [to_z(own_parts[dz], dz) for dz in range(1, n_z)]
    down = after(down, units)
    for dt in range(1, n_tp):
        sources = []
        for arrays in down:
            sources += [to_core(arrays[dt - 1]), arrays[dt - 1]]
        found = run_features(n_tp, n_z, dt, place, units, far_resid, sources)
        parts += [to_z(found[dz], dz, n_tp - dt) for dz in range(n_z)]
    return mix(n_tp, n_z, place, parts).reshape(2, tokens, quarter)


def solution(mesh):
    return jax.shard_map(
        per_device,
        mesh=mesh,
        in_specs=(
            P(None, ("rep", "ep"), "tp"),
            P(None, ("rep", "ep"), "tp"),
            P(None, ("rep", "ep"), None, "tp"),
            P(("rep", "ep"), None, None, "tp"),
            P(("rep", "ep")),
            P("tp", "ep"),
            P("tp", None),
            P("ep", None, "tp", None),
            P(None, ("rep", "ep"), None),
            P(),
            P(),
            P(),
        ),
        out_specs=P(None, ("rep", "ep"), "tp"),
        check_vma=False,
    )
```

```python
import functools
import math

import jax
import jax.numpy as jnp
from jax import lax
from jax.experimental import pallas as pl
from jax.experimental.pallas import tpu as pltpu
from jax.sharding import PartitionSpec as P

HEAD_SIZE = 128
LANES = 128
CORES = 2
MIB = 1 << 20
BF16 = jnp.bfloat16
F32 = jnp.float32
COST = pl.CostEstimate(flops=1000, bytes_accessed=1000, transcendentals=0)


def whole():
    return pl.BlockSpec(memory_space=pltpu.VMEM)


def scalars():
    return pl.BlockSpec(memory_space=pltpu.SMEM)


def unplaced():
    return pl.BlockSpec(memory_space=pltpu.HBM)


def params(mib):
    return pltpu.CompilerParams(vmem_limit_bytes=mib * MIB)


def after(array, earlier):
    return lax.optimization_barrier((array, earlier))[0]


def lookup(entries, wanted_keys):
    return jnp.sum(
        jnp.where(
            wanted_keys[..., None] == jnp.arange(entries.shape[0], dtype=jnp.int32), entries, 0
        ),
        -1,
    )


def slot_tables(old_slots, new_slots, moved_experts):
    slots_all = jnp.arange(old_slots.shape[0], dtype=jnp.int32)
    old_moved = lookup(old_slots, moved_experts)
    new_moved = lookup(new_slots, moved_experts)
    matches = slots_all[:, None] == new_moved[None, :]
    source = jnp.where(
        matches.any(1), jnp.sum(jnp.where(matches, old_moved[None, :], 0), 1), slots_all
    )
    return jnp.stack([old_slots, lookup(source, new_slots)])


def attention_kernel(groups, length_ref, q_ref, cache_ref, fresh_ref, out_ref):
    tokens, width = q_ref.shape[1], q_ref.shape[2]
    rows = 2 * tokens
    context = cache_ref.shape[2]
    heads = width // HEAD_SIZE // groups
    fresh_width = fresh_ref.shape[1] // 2
    length = length_ref[0]
    scale = HEAD_SIZE ** (-0.5) * 1.4426950408889634
    past = lax.broadcasted_iota(jnp.int32, (1, context), 1)
    past_bias = jnp.where(past < length, F32(0.0), F32(-1e30))
    fresh_seen = lax.broadcasted_iota(jnp.int32, (rows, rows), 1) <= (
        lax.broadcasted_iota(jnp.int32, (rows, rows), 0)
    )
    fresh_bias = jnp.where(fresh_seen, F32(0.0), F32(-1e30))
    batch = min(4, heads)
    contract_last = (((1,), (1,)), ((), ()))
    for g in range(groups):
        lanes = pl.ds(g * HEAD_SIZE, HEAD_SIZE)
        past_keys = cache_ref[0, 0, :, lanes]
        past_values = cache_ref[0, 1, :, lanes]
        fresh_keys = fresh_ref[:, lanes]
        fresh_values = fresh_ref[:, pl.ds(fresh_width + g * HEAD_SIZE, HEAD_SIZE)]
        for first in range(0, heads, batch):
            columns = [(g * heads + first + h) * HEAD_SIZE for h in range(batch)]
            q = jnp.concatenate(
                [q_ref[:, :, pl.ds(at, HEAD_SIZE)].reshape(rows, HEAD_SIZE) for at in columns], 0
            )
            past_scores = lax.dot_general(
                q, past_keys, contract_last, preferred_element_type=F32
            ) + past_bias
            fresh_scores = lax.dot_general(
                q, fresh_keys, contract_last, preferred_element_type=F32
            )
            fresh_scores = (
                fresh_scores.reshape(batch, rows, rows) + fresh_bias[None]
            ).reshape(batch * rows, rows)
            largest = jnp.maximum(
                jnp.max(past_scores, 1, keepdims=True), jnp.max(fresh_scores, 1, keepdims=True)
            )
            past_weights = jnp.exp2((past_scores - largest) * scale)
            fresh_weights = jnp.exp2((fresh_scores - largest) * scale)
            total = jnp.sum(past_weights, 1, keepdims=True) + jnp.sum(
                fresh_weights, 1, keepdims=True
            )
            result = jnp.dot(
                past_weights.astype(BF16), past_values, preferred_element_type=F32
            ) + jnp.dot(fresh_weights.astype(BF16), fresh_values, preferred_element_type=F32)
            result = (result / total).astype(BF16)
            for h, at in enumerate(columns):
                out_ref[:, pl.ds(at, HEAD_SIZE)] = result[h * rows : (h + 1) * rows]


def attend(lengths, queries, cache, fresh):
    rows = 2 * queries.shape[1]
    return pl.pallas_call(
        functools.partial(attention_kernel, cache.shape[3] // HEAD_SIZE),
        out_shape=jax.ShapeDtypeStruct((rows, queries.shape[2]), BF16),
        in_specs=[scalars(), whole(), whole(), whole()],
        out_specs=whole(),
        compiler_params=params(40),
        cost_estimate=COST,
        name="attention",
    )(lengths, queries, cache, fresh)


def project_kernel(n_tp, place_ref, *refs):
    t, z_hi = place_ref[0], place_ref[5]
    pieces, weights, out_ref = refs[:n_tp], refs[n_tp:-1], refs[-1]
    chunk = pieces[0].shape[0] // n_tp
    rows = []
    for dt in range(n_tp):
        row = pl.multiple_of(lax.rem(t + dt, n_tp) * chunk, chunk)
        rows += [piece[pl.ds(row, chunk), :] for piece in pieces]
    rows = jnp.concatenate(rows, 0)
    at = 0
    for weight in weights:
        span = weight.shape[1]
        out_ref[:, pl.ds(at, span)] = jnp.dot(rows, weight[...], preferred_element_type=F32)
        at += span


def project(n_tp, place, pieces, weights):
    rows = pieces[0].shape[0] // n_tp * len(pieces) * n_tp
    columns = sum(weight.shape[1] for weight in weights)
    return pl.pallas_call(
        functools.partial(project_kernel, n_tp),
        out_shape=jax.ShapeDtypeStruct((rows, columns), F32),
        in_specs=[scalars()] + [whole()] * (len(pieces) + len(weights)),
        out_specs=whole(),
        compiler_params=params(24),
        cost_estimate=COST,
        name="out_projection",
    )(place, *pieces, *weights)


def finish_kernel(n_tp, spans, place_ref, router_ref, *refs):
    t, core, z_lo, z_hi = place_ref[0], place_ref[2], place_ref[4], place_ref[5]
    pieces, refs = refs[:n_tp], refs[n_tp:]
    weight, early, outs = refs[0], refs[1:-n_tp], refs[-n_tp:]
    chunk = pieces[0].shape[0] // n_tp
    rows = []
    for dt in range(n_tp):
        row = pl.multiple_of(lax.rem(t + dt, n_tp) * chunk, chunk)
        rows += [piece[pl.ds(row, chunk), :] for piece in pieces]
    terms = jnp.dot(jnp.concatenate(rows, 0), weight[...], preferred_element_type=F32)
    for out in outs[1:]:
        out[pl.ds(n_tp * chunk, router_ref.shape[0]), :] = router_ref[...]
    span = weight.shape[1]
    for n in range(spans):
        column = 0
        if spans > 1:
            number = ((z_lo ^ (n // CORES)) * CORES) + (core ^ (n % CORES))
            column = pl.multiple_of(number * span, span)
        for i in range(n_tp * n_tp):
            block = pl.ds(i * chunk, chunk)
            if n + 1 == spans:
                value = terms[i * chunk : (i + 1) * chunk]
            else:
                value = early[0][block, pl.ds(n * span, span)]
            dt, dh = i // n_tp, i % n_tp
            at = pl.multiple_of((z_hi ^ dh) * chunk, chunk)
            outs[dt][pl.ds(at, chunk), pl.ds(column, span)] = value.astype(outs[dt].dtype)


def finish(n_tp, place, router, pieces, weight, early):
    columns = weight.shape[1] + sum(array.shape[1] for array in early)
    spans = columns // weight.shape[1]
    rows = pieces[0].shape[0]
    return pl.pallas_call(
        functools.partial(finish_kernel, n_tp, spans),
        out_shape=[jax.ShapeDtypeStruct((rows, columns), F32)]
        + [jax.ShapeDtypeStruct((rows + router.shape[0], columns), BF16)] * (n_tp - 1),
        in_specs=[scalars()] + [whole()] * (2 + len(pieces) + len(early)),
        out_specs=[whole()] * n_tp,
        compiler_params=params(24),
        cost_estimate=COST,
        name="finish_projection",
    )(place, router, *pieces, weight, *early)


def residual_kernel(n_tp, place_ref, keep_ref, *refs):
    z_hi = place_ref[5]
    terms, hidden, out_ref, marked_ref = refs[: n_tp - 1], refs[n_tp - 1 : -2], refs[-2], refs[-1]
    chunk, columns = hidden[0].shape[0], keep_ref.shape[1]
    for dh, piece in enumerate(hidden):
        rows = pl.ds(pl.multiple_of((z_hi ^ dh) * chunk, chunk), chunk)
        total = keep_ref[rows, :]
        for term in terms:
            total = total + term[rows, :].astype(F32)
        total = (piece[:, pl.ds(0, columns)].astype(F32) + total).astype(BF16)
        out_ref[rows, :] = total
        marked_ref[rows, pl.ds(0, columns)] = total
        lanes = pl.ds(columns, piece.shape[1] - columns)
        marked_ref[rows, lanes] = piece[:, lanes]


def add_residual(n_tp, place, keep, terms, hidden):
    marked = (keep.shape[0], hidden[0].shape[1])
    return pl.pallas_call(
        functools.partial(residual_kernel, n_tp),
        out_shape=[jax.ShapeDtypeStruct(keep.shape, BF16), jax.ShapeDtypeStruct(marked, BF16)],
        in_specs=[scalars()] + [whole()] * (1 + len(terms) + len(hidden)),
        out_specs=[whole()] * 2,
        compiler_params=params(16),
        cost_estimate=COST,
        name="residual",
    )(place, keep, *terms, *hidden)


def hold_kernel(count, *refs):
    token_ref, sems = refs[-2:]
    copies = [
        pltpu.make_async_copy(refs[n], refs[count + n], sems.at[n]) for n in range(count)
    ]
    for copy in copies:
        copy.start()
    token_ref[...] = jnp.zeros_like(token_ref)
    for copy in copies:
        copy.wait()


def hold(arrays):
    found = pl.pallas_call(
        functools.partial(hold_kernel, len(arrays)),
        out_shape=[pltpu.VMEM(array.shape, array.dtype) for array in arrays]
        + [jax.ShapeDtypeStruct((8, LANES), F32)],
        in_specs=[unplaced()] * len(arrays),
        out_specs=[whole()] * (len(arrays) + 1),
        scratch_shapes=[pltpu.SemaphoreType.DMA((len(arrays),))],
        compiler_params=params(2),
        cost_estimate=COST,
        name="hold",
    )(*arrays)
    return found[:-1], found[-1]


def touch_kernel(array_ref, token_ref):
    token_ref[...] = jnp.zeros_like(token_ref)


def touch(array):
    return pl.pallas_call(
        touch_kernel,
        out_shape=jax.ShapeDtypeStruct((8, LANES), F32),
        in_specs=[pl.BlockSpec(memory_space=pl.ANY)],
        out_specs=whole(),
        compiler_params=params(56),
        cost_estimate=COST,
        name="touch",
    )(array)


def units_kernel(n_tp, n_z, n_rep, place_ref, table_ref, *refs):
    t, z, core, rep = place_ref[0], place_ref[1], place_ref[2], place_ref[3]
    z_lo, z_hi = place_ref[4], place_ref[5]
    m = n_z // n_tp
    routers, pieces, refs = refs[:n_tp], refs[n_tp : n_tp + n_z], refs[n_tp + n_z :]
    own_refs, refs = refs[:CORES], refs[CORES:]
    n_far = CORES * (n_tp - 1)
    first_refs, passed_refs, refs = refs[:n_far], refs[n_far : 2 * n_far], refs[2 * n_far :]
    hidden_ref, far_resid_ref, *outs = refs[:-6]
    resid_ref, normed, chosen_ref, total, passed_held, sems = refs[-6:]
    local, _, quarter, units = own_refs[0].shape
    tokens, width = resid_ref.shape
    chunk = tokens // n_z
    experts = routers[0].shape[0]

    arriving = []
    for n in range(n_far):
        copy = pltpu.make_async_copy(passed_refs[n], passed_held.at[n], sems.at[n])
        copy.start()
        arriving.append(copy)

    for dz in range(n_z):
        row = pl.multiple_of((z_lo ^ (dz % m)) * (n_tp * chunk), n_tp * chunk)
        column = pl.multiple_of((z_hi ^ (dz // m)) * quarter, quarter)
        rows = pl.ds(row, n_tp * chunk)
        resid_ref[rows, pl.ds(column, quarter)] = pieces[dz][:, pl.ds(0, quarter)]
        if dz < m:
            chosen_ref[rows, :] = pieces[dz][:, pl.ds(quarter, chosen_ref.shape[1])]
    wide = resid_ref[...].astype(F32)
    squares = jnp.sum(wide * wide, 1, keepdims=True)
    normed[...] = (wide * lax.rsqrt(squares / width + 1e-06)).astype(BF16)
    logits = jnp.zeros((tokens, experts), F32)
    for dt, router in enumerate(routers):
        at = pl.multiple_of(lax.rem(t - dt + n_tp, n_tp) * quarter, quarter)
        logits = logits + lax.dot_general(
            normed[:, pl.ds(at, quarter)],
            router[pl.ds(router.shape[0] - experts, experts), :],
            (((1,), (1,)), ((), ())),
            preferred_element_type=F32,
        )
    chosen = chosen_ref[:, :experts].astype(F32)
    raised = jnp.where(chosen > 0, jnp.exp(logits), F32(0.0))
    combine = raised / jnp.sum(raised, 1, keepdims=True)

    shares = []
    for slot in range(CORES * local):
        other, s = slot // local, slot % local
        holder = jnp.where(core == 0, other, 1 - other)
        number = (z * CORES + holder) * local + s
        shares.append(
            jnp.sum(jnp.where(table_ref[...] == number, combine, F32(0.0)), 1, keepdims=True)
        )
    share = quarter // n_rep
    near = normed[:, pl.ds(pl.multiple_of(t * quarter, quarter), quarter)]
    for other in range(CORES):
        for copy in arriving[other * (n_tp - 1) : (other + 1) * (n_tp - 1)]:
            copy.wait()
        for s in range(local):
            both = []
            for matrix in range(2):
                terms = jnp.dot(near, own_refs[other][s, matrix], preferred_element_type=F32)
                for dt in range(1, n_tp):
                    n = other * (n_tp - 1) + dt - 1
                    base = lax.rem(t - dt + n_tp, n_tp) * quarter
                    for dy, ref in ((0, first_refs[n]), (1, passed_held.at[n])):
                        at = base + lax.rem(rep + dy, n_rep) * share
                        x = normed[:, pl.ds(pl.multiple_of(at, share), share)]
                        terms = terms + jnp.dot(x, ref[s, matrix], preferred_element_type=F32)
                both.append(terms)
            gate, up = both
            acted = (gate / (1.0 + jnp.exp(-gate))) * up
            slot = other * local + s
            hidden_ref[:, pl.ds(slot * units, units)] = (acted * shares[slot]).astype(BF16)

    down = [(own_refs[slot // local], slot % local, 2) for slot in range(CORES * local)]
    lower(down, hidden_ref, total, 0, quarter)
    resid_lanes = pl.ds(pl.multiple_of(t * quarter, quarter), quarter)
    for dz in range(n_z):
        rows = token_rows(z_lo, z_hi, dz, m, n_tp, chunk)
        value = total[rows, :]
        if dz == 0:
            value = value + resid_ref[rows, resid_lanes].astype(F32)
        outs[dz][...] = value.astype(outs[dz].dtype)
    own_rows = token_rows(z_lo, z_hi, 0, m, n_tp, chunk)
    for dt in range(1, n_tp):
        lanes = pl.multiple_of(lax.rem(t - dt + n_tp, n_tp) * quarter, quarter)
        far_resid_ref[dt - 1] = resid_ref[own_rows, pl.ds(lanes, quarter)]


def token_rows(z_lo, z_hi, dz, m, n_tp, chunk):
    at = (z_lo ^ (dz % m)) * n_tp + (z_hi ^ (dz // m))
    return pl.ds(pl.multiple_of(at * chunk, chunk), chunk)


def lower(down, hidden_ref, total, start, width):
    units = hidden_ref.shape[1] // len(down)
    step = min(512, width)
    for at in range(0, width, step):
        size = min(step, width - at)
        part = None
        for i, (ref, *index) in enumerate(down):
            term = lax.dot_general(
                hidden_ref[:, pl.ds(i * units, units)],
                ref[(*index, pl.ds(at, size))],
                (((1,), (1,)), ((), ())),
                preferred_element_type=F32,
            )
            part = term if part is None else part + term
        total[:, pl.ds(start + at, size)] = part


def features_kernel(n_tp, n_z, dt, place_ref, hidden_ref, resid_ref, *refs):
    z_lo, z_hi = place_ref[4], place_ref[5]
    m = n_z // n_tp
    sources, refs = refs[: 2 * CORES], refs[2 * CORES :]
    outs, total, helds, sems = refs[:n_z], refs[n_z], refs[n_z + 1 : -1], refs[-1]
    local = sources[0].shape[0]
    chunk = hidden_ref.shape[0] // n_z
    copies = []
    for n, source in enumerate(sources):
        copy = pltpu.make_async_copy(source, helds[n // CORES].at[n % CORES], sems.at[n])
        copy.start()
        copies.append(copy)
    start = 0
    for n, held in enumerate(helds):
        for copy in copies[n * CORES : (n + 1) * CORES]:
            copy.wait()
        down = [(held.at[slot // local], slot % local, 0) for slot in range(CORES * local)]
        lower(down, hidden_ref, total, start, held.shape[3])
        start += held.shape[3]
    for dz in range(n_z):
        value = total[token_rows(z_lo, z_hi, dz, m, n_tp, chunk), :]
        if dz == 0:
            value = value + resid_ref[dt - 1].astype(F32)
        outs[dz][...] = value.astype(outs[dz].dtype)


def run_units(n_tp, n_rep, place, table, routers, pieces, own, first, passed):
    n_z = len(pieces)
    local, _, quarter, units = own[0].shape
    width = quarter * n_tp
    lanes = pieces[0].shape[1] - quarter
    tokens = pieces[0].shape[0] * (n_z // n_tp)
    part = (tokens // n_z, quarter)
    slots = CORES * local
    n_far = CORES * (n_tp - 1)
    found = pl.pallas_call(
        functools.partial(units_kernel, n_tp, n_z, n_rep),
        out_shape=[
            pltpu.VMEM((tokens, slots * units), BF16),
            jax.ShapeDtypeStruct((n_tp - 1, *part), BF16),
        ]
        + [jax.ShapeDtypeStruct(part, BF16 if dz else F32) for dz in range(n_z)],
        in_specs=[scalars()]
        + [whole()] * (1 + n_tp + len(pieces) + len(own) + len(first))
        + [unplaced()] * n_far,
        out_specs=[whole()] * (2 + n_z),
        scratch_shapes=[
            pltpu.VMEM((tokens, width), BF16),
            pltpu.VMEM((tokens, width), BF16),
            pltpu.VMEM((tokens, lanes), BF16),
            pltpu.VMEM((tokens, quarter), F32),
            pltpu.VMEM((n_far, *passed[0].shape), BF16),
            pltpu.SemaphoreType.DMA((n_far,)),
        ],
        compiler_params=params(28),
        cost_estimate=COST,
        name="units",
    )(place, table, *routers, *pieces, *own, *first, *passed)
    return found[0], found[1], found[2:]


def run_features(n_tp, n_z, dt, place, hidden, resid, weights):
    tokens = hidden.shape[0]
    part = resid.shape[1:]
    return pl.pallas_call(
        functools.partial(features_kernel, n_tp, n_z, dt),
        out_shape=[jax.ShapeDtypeStruct(part, BF16)] * n_z,
        in_specs=[scalars()] + [whole()] * 2 + [unplaced()] * len(weights),
        out_specs=[whole()] * n_z,
        scratch_shapes=[
            pltpu.VMEM((tokens, part[1]), F32),
            *[pltpu.VMEM((CORES, *array.shape), BF16) for array in weights[::CORES]],
            pltpu.SemaphoreType.DMA((len(weights),)),
        ],
        compiler_params=params(16),
        cost_estimate=COST,
        name="features",
    )(place, hidden, resid, *weights)


def message_kernel(n_tp, place_ref, hidden_ref, ids_ref, *refs):
    t, z_hi = place_ref[0], place_ref[5]
    swapped, outs = refs[: n_tp - 1], refs[n_tp - 1 :]
    columns = hidden_ref.shape[1]
    chunk, lanes = outs[0].shape[0], outs[0].shape[1] - columns
    experts = lax.broadcasted_iota(jnp.int32, (chunk, lanes), 1)
    rows = pl.ds(pl.multiple_of(t * chunk, chunk), chunk)
    ids = ids_ref[rows, :]
    found = jnp.zeros((chunk, lanes), F32)
    for k in range(ids.shape[1]):
        found = found + jnp.where(ids[:, k : k + 1] == experts, F32(1.0), F32(0.0))
    for dh, out_ref in enumerate(outs):
        value = hidden_ref[rows, :]
        for dt in range(1, n_tp):
            source = lax.rem(t - dt + n_tp, n_tp)
            value = jnp.where(source == (z_hi ^ dh), swapped[dt - 1][...], value)
        out_ref[:, pl.ds(0, columns)] = value
        out_ref[:, pl.ds(columns, lanes)] = found.astype(BF16)


def messages(n_tp, place, hidden, ids, swapped, experts):
    shape = (ids.shape[0] // n_tp, hidden.shape[1] + experts + -experts % LANES)
    return pl.pallas_call(
        functools.partial(message_kernel, n_tp),
        out_shape=[jax.ShapeDtypeStruct(shape, BF16)] * n_tp,
        in_specs=[scalars()] + [whole()] * (2 + len(swapped)),
        out_specs=[whole()] * n_tp,
        compiler_params=params(16),
        cost_estimate=COST,
        name="messages",
    )(place, hidden, ids, *swapped)


def mix_kernel(n_tp, owners, place_ref, *refs):
    t = place_ref[0]
    parts, out_ref = refs[:-1], refs[-1]
    chunk = parts[0].shape[0]
    for dt in range(n_tp):
        value = None
        for owner, part in zip(owners, parts):
            if owner == dt:
                term = part[...].astype(F32)
                value = term if value is None else value + term
        row = pl.multiple_of(lax.rem(t + dt, n_tp) * chunk, chunk)
        out_ref[pl.ds(row, chunk), :] = value.astype(BF16)


def mix(n_tp, owners, place, parts):
    chunk, span = parts[0].shape
    return pl.pallas_call(
        functools.partial(mix_kernel, n_tp, owners),
        out_shape=jax.ShapeDtypeStruct((chunk * n_tp, span), BF16),
        in_specs=[scalars()] + [whole()] * len(parts),
        out_specs=whole(),
        compiler_params=params(16),
        cost_estimate=COST,
        name="mix",
    )(place, *parts)


def per_device(
    hidden_states,
    queries,
    fresh_key_value,
    cache,
    cache_lengths,
    out_weight,
    router_weight,
    expert_weights,
    expert_ids,
    old_slots,
    new_slots,
    moved_experts,
):
    n_tp, n_ep, n_rep = lax.axis_size("tp"), lax.axis_size("ep"), lax.axis_size("rep")
    n_z = n_ep // CORES
    m = n_z // n_tp
    tokens, quarter = hidden_states.shape[1:]
    rows = 2 * tokens
    chunk = rows // n_tp
    experts = router_weight.shape[1]
    t, e, y = lax.axis_index("tp"), lax.axis_index("ep"), lax.axis_index("rep")
    z, core = e // CORES, e % CORES
    z_hi, z_lo = z // m, z % m
    place = jnp.stack([t, z, core, y, z_lo, z_hi]).astype(jnp.int32)

    def send(array, target):
        pairs = []
        for i in range(n_ep):
            for k in range(n_tp):
                to_ep, to_tp = target(i, k)
                pairs.append((i * n_tp + k, to_ep * n_tp + to_tp % n_tp))
        return lax.ppermute(array, ("ep", "tp"), pairs)

    def to_core(array):
        return lax.ppermute(array, "ep", [(i, i ^ 1) for i in range(n_ep)])

    def to_tp(array, shift):
        return lax.ppermute(array, "tp", [(i, (i + shift) % n_tp) for i in range(n_tp)])

    def to_rep(array, shift):
        return lax.ppermute(array, "rep", [(i, (i + shift) % n_rep) for i in range(n_rep)])

    def to_z(array, dz, dt=0):
        return send(array, lambda i, k: (i ^ (dz * CORES), k + dt))

    def over_z(array, low, high):
        found = {0: array}
        for dz in range(low, high, low):
            step = low
            while not dz & step:
                step *= 2
            found[dz] = to_z(found[dz ^ step], step)
        return [found[dz] for dz in range(0, high, low)]

    def block_of(array, matrices, first_row, size):
        first, last = matrices
        return lax.dynamic_slice(
            array, (0, first, first_row, 0), (array.shape[0], last - first, size, array.shape[3])
        )

    def far(block):
        return [send(block, lambda i, k: (i ^ 1, k + dt)) for dt in range(1, n_tp)]

    flat_hidden = hidden_states.reshape(rows, quarter)
    swapped = [
        to_tp(
            lax.dynamic_slice_in_dim(flat_hidden, lax.rem(t + dt, n_tp) * chunk, chunk, 0), dt
        )
        for dt in range(1, n_tp)
    ]
    near = over_z(out_weight, 1, m)
    out_other = to_core(out_weight)
    share = quarter // n_rep
    first = far(after(block_of(expert_weights, (0, 2), y * share, share), swapped))

    queries = after(queries, (out_other, swapped))
    fresh = fresh_key_value.reshape(rows, -1)
    attention = attend(cache_lengths, queries, cache, fresh)
    pieces = over_z(attention, m, n_z)
    own_other = to_core(expert_weights)
    own_held = touch(after(own_other, attention))
    expert_ids, weights, old_slots, router = after(
        (expert_ids, expert_weights, old_slots, router_weight), (own_held, near)
    )
    outgoing = messages(
        n_tp, place, flat_hidden, expert_ids.reshape(rows, -1), swapped, experts
    )
    edge = 11 * quarter // 16
    blocks = [
        block_of(weights, (2, 3), first_row, last_row - first_row)
        for first_row, last_row in ((0, edge), (edge, quarter))
    ]
    router = router.T
    tables = slot_tables(old_slots, new_slots, moved_experts)
    table = lax.dynamic_slice_in_dim(tables, t * chunk // tokens, 1, 0)
    near, table, router, outgoing, blocks = after(
        (near, table, router, outgoing, blocks), (pieces[1], own_held)
    )
    hidden = [outgoing[0]] + [to_z(outgoing[dh], dh * m) for dh in range(1, n_tp)]
    crossed = [out_other] + [to_core(array) for array in near[1:]]
    early = [array for pair in zip(near, crossed) for array in pair]
    last = early.pop()
    if out_weight.shape[1] % LANES:
        order = (jnp.arange(m)[:, None] ^ z_lo) * CORES + (jnp.arange(CORES) ^ core)
        together = jnp.stack(early + [last])[order.reshape(-1)]
        last, early = together.transpose(1, 0, 2).reshape(together.shape[1], -1), []
    else:
        early = [project(n_tp, place, pieces, early)]
    sums = finish(n_tp, place, router, pieces, last, early)
    terms = [to_tp(sums[dt], dt) for dt in range(1, n_tp)]
    first = after(first, sums)
    passed = [to_rep(array, 1) for array in first]
    first_other = [to_core(array) for array in first]

    resid, marked = add_residual(n_tp, place, sums[0], after(terms, first_other), hidden)
    near = over_z(marked, 1, m)
    wide = to_z(resid, m)
    blocks = after(blocks, resid)
    down = [far(blocks[0])]
    held, all_held = hold(after([expert_weights, own_other] + first_other + first, resid))
    own, held = held[:CORES], held[CORES:]
    wide = after(wide, (near, held[0]))
    gathered = near + [wide]
    for dz in range(m + 1, n_z):
        step = dz & -dz
        gathered.append(to_z(gathered[dz ^ step] if dz ^ step else resid, step))
    gathered, blocks = after((gathered, blocks), (gathered, down))
    down.append(far(blocks[1]))

    passed, down[0] = after((passed, down[0]), gathered)
    passed_other = [to_core(array) for array in passed]
    units, far_resid, own_parts = run_units(
        n_tp,
        n_rep,
        place,
        table,
        [router] + terms,
        gathered,
        own,
        held,
        passed_other + passed,
    )
    order = list(range(m, n_z)) + list(range(1, m)) + [0]
    parts = {(0, dz): to_z(own_parts[dz], dz) if dz else own_parts[0] for dz in order}
    down = after(down, units)
    for dt in range(1, n_tp):
        sources = []
        for arrays in down:
            sources += [to_core(arrays[dt - 1]), arrays[dt - 1]]
        found = run_features(n_tp, n_z, dt, place, units, far_resid, sources)
        for dz in order:
            parts[dt, dz] = to_z(found[dz], dz, n_tp - dt)
    owners = [(dt, dz) for far in (True, False) for dt in range(n_tp) for dz in order if (dz >= m) == far]
    parts = [parts[owner] for owner in owners]
    return mix(n_tp, [dt for dt, _ in owners], place, parts).reshape(2, tokens, quarter)


def solution(mesh):
    return jax.shard_map(
        per_device,
        mesh=mesh,
        in_specs=(
            P(None, ("rep", "ep"), "tp"),
            P(None, ("rep", "ep"), "tp"),
            P(None, ("rep", "ep"), None, "tp"),
            P(("rep", "ep"), None, None, "tp"),
            P(("rep", "ep")),
            P("tp", "ep"),
            P("tp", None),
            P("ep", None, "tp", None),
            P(None, ("rep", "ep"), None),
            P(),
            P(),
            P(),
        ),
        out_specs=P(None, ("rep", "ep"), "tp"),
        check_vma=False,
    )
```
